256 devices in a mesh: rows: 64 (over x, z, core), grp: 4 (over y).
Axes of the slice: x: 4, y: 4, z: 8, core: 2. Of those that a mesh axis runs over, the one named last changes fastest.
Arguments:
- matrix: bfloat16 [262144, 4096], P(('rows', 'grp')), may hold values from -24000 to 24000
- sketch: bfloat16 [4096, 512], P('grp'), may hold values from -0.09375 to 0.09375
Outputs:
- basis_rows: bfloat16 [262144, 512], P(('rows', 'grp'))
- triangle: float32 [512, 512], replicated
- projected: float32 [4096, 512], P(('rows', 'grp'))
The draws below stay inside these ranges and needn't reach their ends.
All inputs are finite; a program needn't handle non-finite values.
Results may differ from the reference program's by a relative error of at most 0.008.
Values may be sent and summed in bfloat16 or wider, within the bound.
No kernel may reach another device: no remote copies, remote signals or barrier semaphores. Data moves between devices by JAX's collectives and lax.ppermute only.
A program may use at most 128 MiB of HBM per device.

```python
import math
import jax
import jax.numpy as jnp
from jax import lax

N = 4096
K = 512
ROW_DEV = 1024
DEVS = 256
ROWS = 262144


def draw_matrix(key, part):
    key = jax.random.fold_in(key, 7)
    subkeys = jax.random.split(key, 5)
    noise_base = jax.random.truncated_normal(subkeys[0], -6.0, 6.0, (ROWS, N), jnp.float32)
    row_span = 10.0
    row_scale = jnp.exp(jax.random.uniform(subkeys[1], (ROWS, 1), jnp.float32, 0.0, math.log(row_span)))
    col_scale = jnp.exp(jax.random.uniform(subkeys[2], (1, N), jnp.float32, 0.0, math.log(10.0)))
    row_trend = jnp.exp(jnp.arange(ROWS, dtype=jnp.float32)[:, None] * (math.log(3.0) / (ROWS - 1)))
    owner = jnp.arange(ROWS) // ROW_DEV
    device_scale = jnp.exp(jax.random.uniform(subkeys[4], (DEVS,), jnp.float32, 0.0, math.log(16.0)))
    block_scale = device_scale[owner][:, None]
    owner_table = jax.random.permutation(subkeys[3], DEVS)
    target = owner_table[owner][:, None]
    col_block = (jnp.arange(N) // (N // DEVS))[None, :]
    source = owner[:, None]
    paired = (target == col_block) | ((source + DEVS // 2) % DEVS == col_block)
    paired = paired | ((source + 1) % DEVS == col_block) | ((source + DEVS - 1) % DEVS == col_block)
    spike_factor = jnp.where(paired, 8.0, 1.0)
    return (0.01 * noise_base * row_scale * row_trend * block_scale * col_scale * spike_factor).astype(jnp.bfloat16)


def block_levels(key, extent, pieces, smallest, top_value):
    def one(dim, shards_of):
        steps = jax.random.uniform(jax.random.fold_in(jax.random.fold_in(key, 6), dim), (shards_of,), jnp.float32, smallest / len(pieces), top_value / len(pieces))
        return jnp.repeat(jnp.exp(steps), extent[dim] // shards_of).reshape((-1,) + (1,) * (len(extent) - dim - 1))

    level = one(*pieces[0])
    for cut in pieces[1:]:
        level = level * one(*cut)
    return level


def bell_draw(key, extent, width, reach, cuts=(), kind=jnp.bfloat16):
    values = jax.random.normal(key, extent, jnp.float32) * width
    if len(cuts) > 0:
        values = block_levels(key, extent, cuts, -0.22, 0.18) * values
    return jnp.clip(values, min=-reach, max=reach).astype(kind)


def setup_inputs(seed: int = 0) -> dict:
    key_list = jax.random.split(jax.random.key(seed), 3)
    matrix = draw_matrix(jax.random.fold_in(key_list[2], 71), 0)
    sketch = bell_draw(key_list[1], (N, K), N ** -0.5, 0.09375, ((0, 4),))
    return dict(matrix=matrix, sketch=sketch)


def reference(matrix, sketch):
    precise = lax.Precision.HIGHEST
    sketched = jnp.dot(matrix.astype(jnp.float32), sketch.astype(jnp.float32), preferred_element_type=jnp.float32)
    gram_total = lax.dot_general(sketched.astype(jnp.float32), sketched.astype(jnp.float32), (((0,), (0,)), ((), ())), precision=precise, preferred_element_type=jnp.float32)
    lower_fac = jnp.linalg.cholesky(gram_total)
    solved = jax.scipy.linalg.solve_triangular(lower_fac, sketched.T, lower=True)
    root_rows = math.sqrt(ROWS)
    basis_rows = (solved.T * root_rows).astype(jnp.bfloat16)
    triangle = lower_fac.T / root_rows
    projected = lax.dot_general(matrix.astype(jnp.float32), basis_rows.astype(jnp.float32), (((0,), (0,)), ((), ())), preferred_element_type=jnp.float32)
    projected = projected * (math.sqrt(N) / ROWS)
    return (basis_rows, triangle, projected)
```

```python
import functools
import math

import jax
import jax.numpy as jnp
from jax import lax
from jax.experimental import pallas as pl
from jax.experimental.pallas import tpu as pltpu
from jax.sharding import PartitionSpec as P

precise = lax.Precision.HIGHEST
BLOCK = 128
TILE = 8
XS, ZS, CORES, YS = 4, 8, 2, 4


def row_pairs(move):
    pairs = []
    for x in range(XS):
        for z in range(ZS):
            for c in range(CORES):
                a, b, d = move(x, z, c)
                pairs.append(((x * ZS + z) * CORES + c, (a * ZS + b) * CORES + d))
    return pairs


def to_core(value):
    return lax.ppermute(value, "rows", row_pairs(lambda x, z, c: (x, z, 1 - c)))


def to_x(value, step):
    return lax.ppermute(value, "rows", row_pairs(lambda x, z, c: ((x + step) % XS, z, c)))


def to_z(value, step):
    return lax.ppermute(value, "rows", row_pairs(lambda x, z, c: (x, (z + step) % ZS, c)))


def to_z_pair(value, bit):
    return lax.ppermute(value, "rows", row_pairs(lambda x, z, c: (x, z ^ bit, c)))


def to_y(value, step):
    return lax.ppermute(value, "grp", [(y, (y + step) % YS) for y in range(YS)])


def take(stack, index, axis=0):
    return lax.dynamic_index_in_dim(stack, index, axis, keepdims=False)


ORDER = (1, 3, 2)


def scatter_sum(stack, place, count, send, axis=0):
    total = take(stack, place, axis)
    for step in ORDER:
        total = total + send(take(stack, lax.rem(place + step, count), axis), step)
    return total


def ring_sum(value, send):
    one, three, two = [send(value, step) for step in ORDER]
    return (value + two) + (one + three)


def lane_splat(tile, lane):
    return jnp.broadcast_to(tile[:, lane : lane + 1], tile.shape)


def row_splat(tile, row):
    return jnp.broadcast_to(tile[row : row + 1, :], tile.shape)


def factor_tile(own, base):
    columns = [lane_splat(own, base + j) for j in range(TILE)]
    a = [[row_splat(columns[j], i) if i >= j else None for j in range(TILE)] for i in range(TILE)]
    low = [[None] * TILE for _ in range(TILE)]
    inv = [None] * TILE
    for j in range(TILE):
        inv[j] = lax.rsqrt(a[j][j])
        for i in range(j + 1, TILE):
            low[i][j] = a[i][j] * inv[j]
        for i in range(j + 1, TILE):
            for k in range(j + 1, i + 1):
                a[i][k] = a[i][k] - low[i][j] * low[k][j]
    return low, inv


def forward(low, inv, tile):
    solved = []
    for j in range(TILE):
        value = row_splat(tile, j)
        for m in range(j):
            value = value - low[j][m] * solved[m]
        solved.append(value * inv[j])
    return solved


def backward(low, inv, rows):
    solved = [None] * TILE
    for j in reversed(range(TILE)):
        value = rows[j]
        for m in range(TILE - 1, j, -1):
            value = value - low[m][j] * solved[m]
        solved[j] = value * inv[j]
    return solved


def factor_block(block):
    count = BLOCK // TILE
    row_id = lax.broadcasted_iota(jnp.int32, (TILE, BLOCK), 0)
    lane_id = lax.broadcasted_iota(jnp.int32, (TILE, BLOCK), 1)

    def merge(rows):
        out = rows[0]
        for j in range(1, TILE):
            out = jnp.where(row_id == j, rows[j], out)
        return out

    left = [block[i * TILE : (i + 1) * TILE, :] for i in range(count)]
    right = [(lane_id == row_id + i * TILE).astype(jnp.float32) for i in range(count)]
    for t in range(count):
        low, inv = factor_tile(left[t], t * TILE)
        rows_left, rows_right = forward(low, inv, left[t]), forward(low, inv, right[t])
        left[t], right[t] = merge(rows_left), merge(rows_right)
        if t + 1 < count:
            back_left, back_right = backward(low, inv, rows_left), backward(low, inv, rows_right)
            for m in range(t + 1, count):
                old = left[m]
                for j in range(TILE):
                    column = lane_splat(old, t * TILE + j)
                    left[m] = left[m] - column * back_left[j]
                    right[m] = right[m] - column * back_right[j]
    upper, inverse = jnp.concatenate(left, 0), jnp.concatenate(right, 0)
    row = lax.broadcasted_iota(jnp.int32, (BLOCK, BLOCK), 0)
    lane = lax.broadcasted_iota(jnp.int32, (BLOCK, BLOCK), 1)
    return jnp.where(lane >= row, upper, 0.0), inverse


def dot(a, b):
    return jnp.dot(a, b, precision=precise, preferred_element_type=jnp.float32)


def dot_first(a, b):
    return lax.dot_general(
        a, b, (((0,), (0,)), ((), ())), precision=precise, preferred_element_type=jnp.float32
    )


def factor_kernel(scale, place_ref, *refs):
    pieces, (tri_ref, inv_ref, packed, work) = refs[:8], refs[8:]
    n = work.shape[0]
    count = n // BLOCK
    piece = pieces[0].shape[0]
    core, y = place_ref[0], place_ref[1]
    for other in range(2):
        half = core if other == 0 else 1 - core
        for slot, step in enumerate((0,) + ORDER):
            start = (half * YS + lax.rem(y - step + YS, YS)) * piece
            packed[pl.ds(pl.multiple_of(start, 8), piece), :] = pieces[other * 4 + slot][...]
    spot = 0
    for i in range(count):
        for j in range(i, count):
            work[i * BLOCK : (i + 1) * BLOCK, j * BLOCK : (j + 1) * BLOCK] = packed[
                spot * BLOCK : (spot + 1) * BLOCK, :
            ]
            spot += 1
    tri_ref[...] = jnp.zeros_like(tri_ref)
    inv_ref[...] = jnp.zeros_like(inv_ref)
    for k in range(count):
        lo, hi = k * BLOCK, (k + 1) * BLOCK
        upper, inverse = factor_block(work[lo:hi, lo:hi])
        tri_ref[lo:hi, lo:hi] = upper * (1.0 / scale)
        if k:
            inv_ref[lo:hi, :lo] = dot(inverse, inv_ref[lo:hi, :lo])
        inv_ref[lo:hi, lo:hi] = inverse * scale
        if hi < n:
            panel = dot(inverse, work[lo:hi, hi:])
            tri_ref[lo:hi, hi:] = panel * (1.0 / scale)
            for i in range(k + 1, count):
                at = (i - k - 1) * BLOCK
                work[i * BLOCK : (i + 1) * BLOCK, i * BLOCK :] -= dot_first(
                    panel[:, at : at + BLOCK], panel[:, at:]
                )
            inv_ref[hi:, :hi] -= dot_first(panel, inv_ref[lo:hi, :hi])


def factor(place, pieces, n, scale):
    whole = jax.ShapeDtypeStruct((n, n), jnp.float32)
    vmem = pl.BlockSpec(memory_space=pltpu.VMEM)
    return pl.pallas_call(
        functools.partial(factor_kernel, scale),
        out_shape=(whole, whole),
        in_specs=[pl.BlockSpec(memory_space=pltpu.SMEM)] + [vmem] * 8,
        out_specs=(vmem, vmem),
        scratch_shapes=[
            pltpu.VMEM((8 * pieces[0].shape[0], BLOCK), jnp.float32),
            pltpu.VMEM((n, n), jnp.float32),
        ],
        compiler_params=pltpu.CompilerParams(vmem_limit_bytes=32 * 2**20),
        cost_estimate=pl.CostEstimate(flops=2 * 10**9, bytes_accessed=4 * 2**20, transcendentals=0),
        name="factor",
    )(place, *pieces)


def on_device(matrix, sketch):
    local_rows, width = matrix.shape
    shard, columns = sketch.shape
    total_rows = local_rows * lax.axis_size(("rows", "grp"))
    place = lax.axis_index("rows")
    y = lax.axis_index("grp")
    core = lax.rem(place, CORES)
    z = lax.rem(lax.div(place, CORES), ZS)
    x = lax.div(place, CORES * ZS)
    z_odd, z_pair = lax.rem(z, 2), lax.div(z, 2)

    half = shard // CORES
    mine = take(sketch.reshape(CORES, half, columns), core)
    arrived = [to_y(mine, step) for step in ORDER]
    passed = [to_core(value) for value in arrived]

    def part(start, rows):
        strip = lax.dynamic_slice_in_dim(matrix, start, rows.shape[0], axis=1)
        return jnp.dot(strip, rows, preferred_element_type=jnp.float32)

    sketched = part(y * shard, sketch)
    for step, near, far in zip(ORDER, arrived, passed):
        source = lax.rem(y + YS - step, YS) * shard
        sketched = sketched + part(source + core * half, near)
        sketched = sketched + part(source + (1 - core) * half, far)

    gram = lax.dot_general(
        sketched,
        sketched,
        (((0,), (0,)), ((), ())),
        precision=precise,
        preferred_element_type=jnp.float32,
    )
    count = columns // BLOCK
    upper = jnp.concatenate(
        [
            gram[i * BLOCK : (i + 1) * BLOCK, j * BLOCK : (j + 1) * BLOCK]
            for i in range(count)
            for j in range(i, count)
        ],
        axis=0,
    ).reshape(CORES, -1, BLOCK)
    summed = take(upper, core) + to_core(take(upper, 1 - core))
    summed = scatter_sum(summed.reshape(YS, -1, BLOCK), y, YS, to_y)
    summed = ring_sum(summed, to_x)
    summed = summed + to_z_pair(summed, 1)
    summed = ring_sum(summed, lambda value, step: to_z(value, 2 * step))
    pieces = [summed] + [to_y(summed, step) for step in ORDER]
    pieces = pieces + [to_core(value) for value in pieces]
    root_rows = math.sqrt(total_rows)
    triangle, inverse = factor(
        jnp.stack([core, y]).astype(jnp.int32), pieces, columns, root_rows
    )

    high = sketched.astype(jnp.bfloat16)
    rest = (sketched - high.astype(jnp.float32)).astype(jnp.bfloat16)

    def product(which):
        wide = columns // CORES
        out = 0.0
        for piece in (high, rest):
            strip = lax.dynamic_slice_in_dim(piece, which * wide, wide, axis=1)
            out = out + lax.dot_general(
                strip, matrix, (((0,), (0,)), ((), ())), preferred_element_type=jnp.float32
            )
        return out

    merged = product(core) + to_core(product(1 - core))
    rows_half = columns // CORES // 2
    first, second = merged[:rows_half], merged[rows_half:]
    first = scatter_sum(first.reshape(rows_half, XS, -1), x, XS, to_x, axis=1)
    second = scatter_sum(second.reshape(YS, rows_half // YS, -1), y, YS, to_y)
    first = scatter_sum(first.reshape(YS, rows_half // YS, -1), y, YS, to_y)
    second = scatter_sum(second.reshape(rows_half // YS, XS, -1), x, XS, to_x, axis=1)
    both = jnp.concatenate([first, second], axis=0)
    deep = both.shape[0]
    both = both.reshape(deep, ZS // 2, 2, -1)
    both = take(both, z_odd, 2) + to_z_pair(take(both, 1 - z_odd, 2), 1)
    both = scatter_sum(
        both, z_pair, ZS // 2, lambda value, step: to_z(value, 2 * step), axis=1
    )
    own = width // (XS * ZS * CORES * YS)
    turned = both.T.reshape(CORES, YS, own, deep)
    sent = [take(turned, lax.rem(y + step, YS), 1) for step in (0,) + ORDER]
    got = [sent[0]] + [to_y(value, step) for step, value in zip(ORDER, sent[1:])]
    stack = jnp.stack([got[0], got[1], got[3], got[2]], axis=0)
    ordered = jnp.stack([take(stack, lax.rem(y + YS - j, YS)) for j in range(YS)], axis=0)
    kept = take(ordered, core, 1)
    swapped = to_core(take(ordered, 1 - core, 1))
    pair = jnp.stack([jnp.where(core == 0, kept, swapped), jnp.where(core == 0, swapped, kept)])
    pair = pair.reshape(CORES, YS, own, 2, deep // 2)
    strip = jnp.transpose(pair, (2, 0, 3, 1, 4)).reshape(own, columns)

    def through(value):
        return lax.dot_general(
            value,
            inverse,
            (((1,), (1,)), ((), ())),
            precision=precise,
            preferred_element_type=jnp.float32,
        )

    basis_block = through(sketched).astype(jnp.bfloat16)
    projected = through(strip) * (math.sqrt(width) / total_rows)
    return (basis_block, triangle, projected)


def solution(mesh):
    return jax.shard_map(
        on_device,
        mesh=mesh,
        in_specs=(P(("rows", "grp"), None), P("grp", None)),
        out_specs=(P(("rows", "grp"), None), P(), P(("rows", "grp"), None)),
        check_vma=False,
    )
```

```python
import functools
import math

import jax
import jax.numpy as jnp
from jax import lax
from jax.experimental import pallas as pl
from jax.experimental.pallas import tpu as pltpu
from jax.sharding import PartitionSpec as P

precise = lax.Precision.HIGHEST
BLOCK = 128
TILE = 8
XS, ZS, CORES, YS = 4, 8, 2, 4


def row_pairs(move):
    pairs = []
    for x in range(XS):
        for z in range(ZS):
            for c in range(CORES):
                a, b, d = move(x, z, c)
                pairs.append(((x * ZS + z) * CORES + c, (a * ZS + b) * CORES + d))
    return pairs


def to_core(value):
    return lax.ppermute(value, "rows", row_pairs(lambda x, z, c: (x, z, 1 - c)))


def to_x(value, step):
    return lax.ppermute(value, "rows", row_pairs(lambda x, z, c: ((x + step) % XS, z, c)))


def to_z(value, step):
    return lax.ppermute(
        value, "rows", row_pairs(lambda x, z, c: (x, z // 4 * 4 + (z + step) % 4, c))
    )


def to_z_half(value):
    return lax.ppermute(value, "rows", row_pairs(lambda x, z, c: (x, (z + 4) % ZS, c)))


def to_y(value, step):
    return lax.ppermute(value, "grp", [(y, (y + step) % YS) for y in range(YS)])


def take(stack, index, axis=0):
    return lax.dynamic_index_in_dim(stack, index, axis, keepdims=False)


ORDER = (1, 3, 2)


def cut(value, index, count, axis):
    size = value.shape[axis] // count
    return lax.dynamic_slice_in_dim(value, index * size, size, axis=axis)


def scatter_sum(value, place, count, send, axis=0):
    total = cut(value, place, count, axis)
    for step in ORDER:
        total = total + send(cut(value, lax.rem(place + step, count), count, axis), step)
    return total


def ring_sum(value, send):
    one, three, two = [send(value, step) for step in ORDER]
    return (value + two) + (one + three)


def lane_splat(tile, lane):
    return jnp.broadcast_to(tile[:, lane : lane + 1], tile.shape)


def row_splat(tile, row):
    return jnp.broadcast_to(tile[row : row + 1, :], tile.shape)


def factor_tile(own, base):
    columns = [lane_splat(own, base + j) for j in range(TILE)]
    a = [[row_splat(columns[j], i) if i >= j else None for j in range(TILE)] for i in range(TILE)]
    low = [[None] * TILE for _ in range(TILE)]
    inv = [None] * TILE
    for j in range(TILE):
        inv[j] = lax.rsqrt(a[j][j])
        for i in range(j + 1, TILE):
            low[i][j] = a[i][j] * inv[j]
        for i in range(j + 1, TILE):
            for k in range(j + 1, i + 1):
                a[i][k] = a[i][k] - low[i][j] * low[k][j]
    return low, inv


def forward(low, inv, tile):
    solved = []
    for j in range(TILE):
        value = row_splat(tile, j)
        for m in range(j):
            value = value - low[j][m] * solved[m]
        solved.append(value * inv[j])
    return solved


def backward(low, inv, rows):
    solved = [None] * TILE
    for j in reversed(range(TILE)):
        value = rows[j]
        for m in range(TILE - 1, j, -1):
            value = value - low[m][j] * solved[m]
        solved[j] = value * inv[j]
    return solved


def factor_block(block):
    count = BLOCK // TILE
    row_id = lax.broadcasted_iota(jnp.int32, (TILE, BLOCK), 0)
    lane_id = lax.broadcasted_iota(jnp.int32, (TILE, BLOCK), 1)

    def merge(rows):
        out = rows[0]
        for j in range(1, TILE):
            out = jnp.where(row_id == j, rows[j], out)
        return out

    left = [block[i * TILE : (i + 1) * TILE, :] for i in range(count)]
    right = [(lane_id == row_id + i * TILE).astype(jnp.float32) for i in range(count)]
    for t in range(count):
        low, inv = factor_tile(left[t], t * TILE)
        rows_left, rows_right = forward(low, inv, left[t]), forward(low, inv, right[t])
        left[t], right[t] = merge(rows_left), merge(rows_right)
        if t + 1 < count:
            back_left, back_right = backward(low, inv, rows_left), backward(low, inv, rows_right)
            for m in range(t + 1, count):
                old = left[m]
                for j in range(TILE):
                    column = lane_splat(old, t * TILE + j)
                    left[m] = left[m] - column * back_left[j]
                    right[m] = right[m] - column * back_right[j]
    upper, inverse = jnp.concatenate(left, 0), jnp.concatenate(right, 0)
    row = lax.broadcasted_iota(jnp.int32, (BLOCK, BLOCK), 0)
    lane = lax.broadcasted_iota(jnp.int32, (BLOCK, BLOCK), 1)
    return jnp.where(lane >= row, upper, 0.0), inverse


def dot(a, b):
    return jnp.dot(a, b, precision=precise, preferred_element_type=jnp.float32)


def dot_first(a, b):
    return lax.dot_general(
        a, b, (((0,), (0,)), ((), ())), precision=precise, preferred_element_type=jnp.float32
    )


HALVES = (((0, 0), (0, 1), (0, 2), (0, 3), (3, 3)), ((1, 1), (1, 2), (1, 3), (2, 2), (2, 3)))


def span(index):
    return slice(index * BLOCK, (index + 1) * BLOCK)


def gram_kernel(place_ref, mine_ref, other_ref, *refs):
    outs, stack_ref, packed = refs[:4], refs[4], refs[5]
    core, y = place_ref[0], place_ref[1]
    rows = mine_ref.shape[0]
    for half in range(2):

        @pl.when(core == half)
        def _():
            spot = 0
            for i in sorted({i for i, _ in HALVES[half]}):
                lanes = [j for k, j in HALVES[half] if k == i]
                wide = slice(lanes[0] * BLOCK, (lanes[-1] + 1) * BLOCK)
                strip = sum(
                    dot_first(ref[:, span(i)], ref[:, wide]) for ref in (mine_ref, other_ref)
                )
                for at in range(len(lanes)):
                    packed[span(spot), :] = strip[:, span(at)]
                    spot += 1

    piece = outs[0].shape[0]
    for out, step in zip(outs, (0,) + ORDER):
        start = lax.rem(y + step, YS) * piece
        out[...] = packed[pl.ds(pl.multiple_of(start, 8), piece), :]
    wide = stack_ref.shape[0] // 2
    for at, ref in enumerate((mine_ref, other_ref)):
        turned = ref[:, pl.ds(pl.multiple_of(core * wide, wide), wide)].T
        high = turned.astype(jnp.bfloat16)
        lanes = slice(at * rows, (at + 1) * rows)
        stack_ref[:wide, lanes] = high
        stack_ref[wide:, lanes] = (turned - high.astype(jnp.float32)).astype(jnp.bfloat16)


def gram_pieces(place, mine, other):
    rows, columns = mine.shape
    piece = 5 * BLOCK // YS
    vmem = pl.BlockSpec(memory_space=pltpu.VMEM)
    return pl.pallas_call(
        gram_kernel,
        out_shape=[jax.ShapeDtypeStruct((piece, BLOCK), jnp.float32)] * 4
        + [jax.ShapeDtypeStruct((columns, 2 * rows), jnp.bfloat16)],
        in_specs=[pl.BlockSpec(memory_space=pltpu.SMEM), vmem, vmem],
        out_specs=[vmem] * 5,
        scratch_shapes=[pltpu.VMEM((5 * BLOCK, BLOCK), jnp.float32)],
        compiler_params=pltpu.CompilerParams(vmem_limit_bytes=40 * 2**20),
        cost_estimate=pl.CostEstimate(
            flops=2 * 10**9, bytes_accessed=8 * 2**20, transcendentals=0
        ),
        name="gram",
    )(place, mine, other)


SEND = ORDER + (0,)


def product_kernel(place_ref, stack_ref, mine_ref, other_ref, *refs):
    over_x, over_y, held = refs[:4], refs[4:8], refs[8]
    step = pl.program_id(0)
    y, x = place_ref[1], place_ref[2]
    rows, wide = mine_ref.shape
    half = stack_ref.shape[0] // 2
    both = jnp.dot(stack_ref[:, :rows], mine_ref[...], preferred_element_type=jnp.float32)
    both += jnp.dot(stack_ref[:, rows:], other_ref[...], preferred_element_type=jnp.float32)
    value = both[:half] + both[half:]
    top = half // 2
    for at in range(4):

        @pl.when(step == at)
        def _():
            over_x[at][...] = value[:top]

    held[...] = value[top:]
    shift = jnp.where(step == 0, SEND[0], jnp.where(step == 1, SEND[1], jnp.where(step == 2, SEND[2], SEND[3])))
    lanes = pl.ds(pl.multiple_of(lax.rem(x + shift, XS) * wide, wide), wide)
    size = top // YS
    for at in range(4):
        start = lax.rem(y + SEND[at], YS) * size
        over_y[at][:, lanes] = held[pl.ds(pl.multiple_of(start, 8), size), :]


def product(place, stack, mine, other):
    rows, width = mine.shape
    columns = stack.shape[0]
    wide, top = width // XS, columns // 4

    def chunk(step, place_ref):
        shift = jnp.where(step == 0, SEND[0], jnp.where(step == 1, SEND[1], jnp.where(step == 2, SEND[2], SEND[3])))
        return (0, lax.rem(place_ref[2] + shift, XS))

    def whole(*shape):
        return pl.BlockSpec(shape, lambda step, place_ref: (0, 0))

    return pl.pallas_call(
        product_kernel,
        grid_spec=pltpu.PrefetchScalarGridSpec(
            num_scalar_prefetch=1,
            grid=(XS,),
            in_specs=[
                whole(*stack.shape),
                pl.BlockSpec((rows, wide), chunk),
                pl.BlockSpec((rows, wide), chunk),
            ],
            out_specs=[whole(top, wide)] * 4 + [whole(top // YS, width)] * 4,
            scratch_shapes=[pltpu.VMEM((top, wide), jnp.float32)],
        ),
        out_shape=[jax.ShapeDtypeStruct((top, wide), jnp.float32)] * 4
        + [jax.ShapeDtypeStruct((top // YS, width), jnp.float32)] * 4,
        compiler_params=pltpu.CompilerParams(vmem_limit_bytes=40 * 2**20),
        cost_estimate=pl.CostEstimate(
            flops=8 * rows * width * columns // 2, bytes_accessed=22 * 2**20, transcendentals=0
        ),
        name="product",
    )(place, stack, mine, other)


def factor_steps(scale, first, last, tri_ref, inv_ref, work):
    n = work.shape[0]
    count = n // BLOCK
    for k in range(first, last):
        lo, hi = k * BLOCK, (k + 1) * BLOCK
        upper, inverse = factor_block(work[lo:hi, lo:hi])
        tri_ref[lo:hi, lo:hi] = upper * (1.0 / scale)
        if k:
            inv_ref[lo:hi, :lo] = dot(inverse, inv_ref[lo:hi, :lo])
        inv_ref[lo:hi, lo:hi] = inverse * scale
        if hi < n:
            panel = dot(inverse, work[lo:hi, hi:])
            tri_ref[lo:hi, hi:] = panel * (1.0 / scale)
            for i in range(k + 1, count):
                at = (i - k - 1) * BLOCK
                work[i * BLOCK : (i + 1) * BLOCK, i * BLOCK :] -= dot_first(
                    panel[:, at : at + BLOCK], panel[:, at:]
                )
            inv_ref[hi:, :hi] -= dot_first(panel, inv_ref[lo:hi, :hi])


def factor_first(scale, middle, place_ref, *refs):
    pieces, (tri_ref, inv_ref, work, packed) = refs[:8], refs[8:]
    piece = pieces[0].shape[0]
    core, y = place_ref[0], place_ref[1]
    for other in range(2):
        half = core if other == 0 else 1 - core
        for slot, step in enumerate((0,) + ORDER):
            start = (half * YS + lax.rem(y - step + YS, YS)) * piece
            packed[pl.ds(pl.multiple_of(start, 8), piece), :] = pieces[other * 4 + slot][...]
    for spot, (i, j) in enumerate(HALVES[0] + HALVES[1]):
        work[span(i), span(j)] = packed[span(spot), :]
    for i in range(1, work.shape[0] // BLOCK):
        work[span(i), : i * BLOCK] = jnp.zeros((BLOCK, i * BLOCK), jnp.float32)
    tri_ref[...] = jnp.zeros_like(tri_ref)
    inv_ref[...] = jnp.zeros_like(inv_ref)
    factor_steps(scale, 0, middle, tri_ref, inv_ref, work)


def factor_second(scale, middle, tri_in, inv_in, work_in, after, tri_ref, inv_ref, work):
    tri_ref[...] = tri_in[...]
    inv_ref[...] = inv_in[...]
    work[...] = work_in[...]
    factor_steps(scale, middle, work.shape[0] // BLOCK, tri_ref, inv_ref, work)


def factor_begin(place, pieces, n, scale, middle):
    whole = jax.ShapeDtypeStruct((n, n), jnp.float32)
    vmem = pl.BlockSpec(memory_space=pltpu.VMEM)
    return pl.pallas_call(
        functools.partial(factor_first, scale, middle),
        out_shape=(whole,) * 3,
        in_specs=[pl.BlockSpec(memory_space=pltpu.SMEM)] + [vmem] * 8,
        out_specs=(vmem,) * 3,
        scratch_shapes=[pltpu.VMEM((8 * pieces[0].shape[0], BLOCK), jnp.float32)],
        compiler_params=pltpu.CompilerParams(vmem_limit_bytes=32 * 2**20),
        cost_estimate=pl.CostEstimate(
            flops=12 * 10**9, bytes_accessed=4 * 2**20, transcendentals=0
        ),
        name="factor_begin",
    )(place, *pieces)


def factor_end(parts, after, n, scale, middle):
    whole = jax.ShapeDtypeStruct((n, n), jnp.float32)
    vmem = pl.BlockSpec(memory_space=pltpu.VMEM)
    return pl.pallas_call(
        functools.partial(factor_second, scale, middle),
        out_shape=(whole,) * 2,
        in_specs=[vmem] * 3 + [pl.BlockSpec(memory_space=pl.ANY)],
        out_specs=(vmem,) * 2,
        scratch_shapes=[pltpu.VMEM((n, n), jnp.float32)],
        compiler_params=pltpu.CompilerParams(vmem_limit_bytes=32 * 2**20),
        cost_estimate=pl.CostEstimate(
            flops=12 * 10**9, bytes_accessed=4 * 2**20, transcendentals=0
        ),
        name="factor_end",
    )(*parts, after)


def on_device(matrix, sketch):
    local_rows, width = matrix.shape
    shard, columns = sketch.shape
    total_rows = local_rows * lax.axis_size(("rows", "grp"))
    rows_place = lax.axis_index("rows")
    y = lax.axis_index("grp")
    core = lax.rem(rows_place, CORES)
    z = lax.rem(lax.div(rows_place, CORES), ZS)
    x = lax.div(rows_place, CORES * ZS)
    z_half, z_low = lax.div(z, 4), lax.rem(z, 4)
    place = jnp.stack([core, y, x]).astype(jnp.int32)

    half = shard // CORES
    mine = cut(sketch, core, CORES, 0)
    arrived = [to_y(mine, step) for step in ORDER]
    other_matrix = to_core(matrix)
    passed = [to_core(value) for value in arrived]

    def sketch_rows(rows):
        def part(start, value):
            strip = lax.dynamic_slice_in_dim(rows, start, value.shape[0], axis=1)
            return jnp.dot(strip, value, preferred_element_type=jnp.float32)

        out = part(y * shard, sketch)
        for step, near, far in zip(ORDER, arrived, passed):
            source = lax.rem(y + YS - step, YS) * shard
            out = out + part(source + core * half, near)
            out = out + part(source + (1 - core) * half, far)
        return out

    sketched, other_sketched = sketch_rows(matrix), sketch_rows(other_matrix)
    *gram, stack = gram_pieces(place, sketched, other_sketched)

    summed = gram[0]
    for step, value in zip(ORDER, gram[1:]):
        summed = summed + to_y(value, step)
    summed = ring_sum(summed, to_x)
    summed = summed + to_z_half(summed)
    summed = ring_sum(summed, to_z)
    pieces = [summed] + [to_y(summed, step) for step in ORDER]
    pieces = pieces + [to_core(value) for value in pieces]

    parts = product(place, stack, matrix, other_matrix)
    moved = [to_x(parts[at], step) for at, step in enumerate(ORDER)]
    moved += [to_y(parts[4 + at], step) for at, step in enumerate(ORDER)]
    first, second = parts[3], parts[7]
    for at in range(3):
        first, second = first + moved[at], second + moved[3 + at]
    first = scatter_sum(first, y, YS, to_y)
    second = scatter_sum(second, x, XS, to_x, axis=1)
    both = jnp.concatenate([first, second], axis=0)
    both = cut(both, z_half, 2, 1) + to_z_half(cut(both, 1 - z_half, 2, 1))
    both = scatter_sum(both, z_low, 4, to_z, axis=1)

    deep = both.shape[0]
    own = width // (XS * ZS * CORES * YS)
    turned = both.T.reshape(CORES, YS, own, deep)

    def take(stack, index, axis=0):
        return lax.dynamic_index_in_dim(stack, index, axis, keepdims=False)

    got = [take(turned, y, 1)]
    got += [to_y(take(turned, lax.rem(y + step, YS), 1), step) for step in ORDER]
    stacked = jnp.stack([got[0], got[1], got[3], got[2]], axis=0)
    ordered = jnp.stack([take(stacked, lax.rem(y + YS - j, YS)) for j in range(YS)], axis=0)
    kept = take(ordered, core, 1)
    swapped = to_core(take(ordered, 1 - core, 1))
    pair = jnp.stack([jnp.where(core == 0, kept, swapped), jnp.where(core == 0, swapped, kept)])
    pair = pair.reshape(CORES, YS, own, 2, deep // 2)
    strip = jnp.transpose(pair, (2, 0, 3, 1, 4)).reshape(own, columns)

    root_rows = math.sqrt(total_rows)
    begun = factor_begin(place, pieces, columns, root_rows, 2)
    triangle, inverse = factor_end(begun, both, columns, root_rows, 2)

    def through(value):
        return lax.dot_general(
            value,
            inverse,
            (((1,), (1,)), ((), ())),
            precision=precise,
            preferred_element_type=jnp.float32,
        )

    basis_block = through(sketched).astype(jnp.bfloat16)
    projected = through(strip) * (math.sqrt(width) / total_rows)
    return (basis_block, triangle, projected)


def solution(mesh):
    return jax.shard_map(
        on_device,
        mesh=mesh,
        in_specs=(P(("rows", "grp"), None), P("grp", None)),
        out_specs=(P(("rows", "grp"), None), P(), P(("rows", "grp"), None)),
        check_vma=False,
    )
```

```python
import functools
import math

import jax
import jax.numpy as jnp
from jax import lax
from jax.experimental import pallas as pl
from jax.experimental.pallas import tpu as pltpu
from jax.sharding import PartitionSpec as P

precise = lax.Precision.HIGHEST
BLOCK = 128
TILE = 8
XS, ZS, CORES, YS = 4, 8, 2, 4


def row_pairs(move):
    pairs = []
    for x in range(XS):
        for z in range(ZS):
            for c in range(CORES):
                a, b, d = move(x, z, c)
                pairs.append(((x * ZS + z) * CORES + c, (a * ZS + b) * CORES + d))
    return pairs


def to_core(value):
    return lax.ppermute(value, "rows", row_pairs(lambda x, z, c: (x, z, 1 - c)))


def to_x(value, step):
    return lax.ppermute(value, "rows", row_pairs(lambda x, z, c: (x ^ step, z, c)))


def to_z(value, step):
    return lax.ppermute(value, "rows", row_pairs(lambda x, z, c: (x, z ^ (2 * step), c)))


def to_z_pair(value):
    return lax.ppermute(value, "rows", row_pairs(lambda x, z, c: (x, z ^ 1, c)))


def to_y(value, step):
    return lax.ppermute(value, "grp", [(y, y ^ step) for y in range(YS)])


ORDER = (1, 3, 2)


def cut(value, index, count, axis):
    size = value.shape[axis] // count
    return lax.dynamic_slice_in_dim(value, index * size, size, axis=axis)


def scatter_sum(value, place, count, send, axis=0):
    total = cut(value, place, count, axis)
    for step in ORDER:
        total = total + send(cut(value, place ^ step, count, axis), step)
    return total


def ring_sum(value, send):
    one, three, two = [send(value, step) for step in ORDER]
    return (value + two) + (one + three)


def lane_splat(tile, lane):
    return jnp.broadcast_to(tile[:, lane : lane + 1], tile.shape)


def row_splat(tile, row):
    return jnp.broadcast_to(tile[row : row + 1, :], tile.shape)


def factor_tile(own, base):
    columns = [lane_splat(own, base + j) for j in range(TILE)]
    a = [[row_splat(columns[j], i) if i >= j else None for j in range(TILE)] for i in range(TILE)]
    low = [[None] * TILE for _ in range(TILE)]
    inv = [None] * TILE
    for j in range(TILE):
        inv[j] = lax.rsqrt(a[j][j])
        for i in range(j + 1, TILE):
            low[i][j] = a[i][j] * inv[j]
        for i in range(j + 1, TILE):
            for k in range(j + 1, i + 1):
                a[i][k] = a[i][k] - low[i][j] * low[k][j]
    return low, inv


def forward(low, inv, tile):
    solved = []
    for j in range(TILE):
        value = row_splat(tile, j)
        for m in range(j):
            value = value - low[j][m] * solved[m]
        solved.append(value * inv[j])
    return solved


def backward(low, inv, rows):
    solved = [None] * TILE
    for j in reversed(range(TILE)):
        value = rows[j]
        for m in range(TILE - 1, j, -1):
            value = value - low[m][j] * solved[m]
        solved[j] = value * inv[j]
    return solved


def factor_block(block):
    count = BLOCK // TILE
    row_id = lax.broadcasted_iota(jnp.int32, (TILE, BLOCK), 0)
    lane_id = lax.broadcasted_iota(jnp.int32, (TILE, BLOCK), 1)

    def merge(rows):
        out = rows[0]
        for j in range(1, TILE):
            out = jnp.where(row_id == j, rows[j], out)
        return out

    left = [block[i * TILE : (i + 1) * TILE, :] for i in range(count)]
    right = [(lane_id == row_id + i * TILE).astype(jnp.float32) for i in range(count)]
    for t in range(count):
        low, inv = factor_tile(left[t], t * TILE)
        rows_left, rows_right = forward(low, inv, left[t]), forward(low, inv, right[t])
        left[t], right[t] = merge(rows_left), merge(rows_right)
        if t + 1 < count:
            back_left, back_right = backward(low, inv, rows_left), backward(low, inv, rows_right)
            for m in range(t + 1, count):
                old = left[m]
                for j in range(TILE):
                    column = lane_splat(old, t * TILE + j)
                    left[m] = left[m] - column * back_left[j]
                    right[m] = right[m] - column * back_right[j]
    upper, inverse = jnp.concatenate(left, 0), jnp.concatenate(right, 0)
    row = lax.broadcasted_iota(jnp.int32, (BLOCK, BLOCK), 0)
    lane = lax.broadcasted_iota(jnp.int32, (BLOCK, BLOCK), 1)
    return jnp.where(lane >= row, upper, 0.0), inverse


def dot(a, b):
    return jnp.dot(a, b, precision=precise, preferred_element_type=jnp.float32)


def dot_first(a, b):
    return lax.dot_general(
        a, b, (((0,), (0,)), ((), ())), precision=precise, preferred_element_type=jnp.float32
    )


HALVES = (((0, 0), (0, 1), (0, 2), (0, 3), (3, 3)), ((1, 1), (1, 2), (1, 3), (2, 2), (2, 3)))


def span(index):
    return slice(index * BLOCK, (index + 1) * BLOCK)


def gram_kernel(place_ref, rows_ref, keep_ref, send_ref, *refs):
    stacks, packed = refs[:-1], refs[-1]
    core = place_ref[0]
    spot = 0
    for half in range(2):
        for i in sorted({i for i, _ in HALVES[half]}):
            lanes = [j for k, j in HALVES[half] if k == i]
            wide = slice(lanes[0] * BLOCK, (lanes[-1] + 1) * BLOCK)
            strip = dot_first(rows_ref[:, span(i)], rows_ref[:, wide])
            for at in range(len(lanes)):
                packed[span(spot), :] = strip[:, span(at)]
                spot += 1
    size = keep_ref.shape[0]
    keep_ref[...] = packed[pl.ds(pl.multiple_of(core * size, size), size), :]
    send_ref[...] = packed[pl.ds(pl.multiple_of((1 - core) * size, size), size), :]
    start = 0
    for stack_ref in stacks:
        wide = stack_ref.shape[0] // 2
        turned = rows_ref[:, start : start + wide].T
        high = turned.astype(jnp.bfloat16)
        stack_ref[:wide, :] = high
        stack_ref[wide:, :] = (turned - high.astype(jnp.float32)).astype(jnp.bfloat16)
        start += wide


def gram_pieces(place, sketched, widths):
    rows, columns = sketched.shape
    size = 5 * BLOCK
    vmem = pl.BlockSpec(memory_space=pltpu.VMEM)
    return pl.pallas_call(
        gram_kernel,
        out_shape=[jax.ShapeDtypeStruct((size, BLOCK), jnp.float32)] * 2
        + [jax.ShapeDtypeStruct((2 * wide, rows), jnp.bfloat16) for wide in widths],
        in_specs=[pl.BlockSpec(memory_space=pltpu.SMEM), vmem],
        out_specs=[vmem] * (2 + len(widths)),
        scratch_shapes=[pltpu.VMEM((2 * size, BLOCK), jnp.float32)],
        compiler_params=pltpu.CompilerParams(vmem_limit_bytes=40 * 2**20),
        cost_estimate=pl.CostEstimate(
            flops=2 * 10**9, bytes_accessed=8 * 2**20, transcendentals=0
        ),
        name="gram",
    )(place, sketched)


SEND = ORDER + (0,)


def product_kernel(own, place_ref, stack_ref, strip_ref, keep_ref, send_ref, held):
    core = place_ref[0]
    half = stack_ref.shape[0] // 2
    both = jnp.dot(stack_ref[...], strip_ref[...], preferred_element_type=jnp.float32)
    held[...] = (both[:half] + both[half:]).T
    for c in range(CORES):
        for wanted, out in ((core == c, keep_ref), (core != c, send_ref)):

            @pl.when(wanted)
            def _():
                for y in range(YS):
                    for z in range(ZS):
                        start = ((z * CORES + c) * YS + y) * own
                        spot = (y * ZS + z) * own
                        out[spot : spot + own, :] = held[start : start + own, :]


def product(place, stack, matrix, step):
    rows, width = matrix.shape
    wide = stack.shape[0] // 2
    strip = width // XS
    own = strip // (ZS * CORES * YS)
    out = pl.BlockSpec((strip // CORES, wide), lambda i, place_ref: (0, 0))
    return pl.pallas_call(
        functools.partial(product_kernel, own),
        grid_spec=pltpu.PrefetchScalarGridSpec(
            num_scalar_prefetch=1,
            grid=(1,),
            in_specs=[
                pl.BlockSpec(stack.shape, lambda i, place_ref: (0, 0)),
                pl.BlockSpec((rows, strip), lambda i, place_ref: (0, place_ref[2] ^ step)),
            ],
            out_specs=[out] * 2,
            scratch_shapes=[pltpu.VMEM((strip, wide), jnp.float32)],
        ),
        out_shape=[jax.ShapeDtypeStruct((strip // CORES, wide), jnp.float32)] * 2,
        compiler_params=pltpu.CompilerParams(vmem_limit_bytes=40 * 2**20),
        cost_estimate=pl.CostEstimate(
            flops=4 * rows * strip * wide, bytes_accessed=6 * 2**20, transcendentals=0
        ),
        name="product",
    )(place, stack, matrix)


def merge_kernel(place_ref, *refs):
    keeps, others, over_x, over_y = refs[:4], refs[4:8], refs[8:12], refs[12:16]
    y = place_ref[1]
    wide = over_x[0].shape[1]
    size = over_x[0].shape[0] // YS
    for at in range(XS):
        over_x[at][...] = keeps[at][:, :wide] + others[at][:, :wide]
        for out, step in zip(over_y, SEND):
            rows = pl.ds(pl.multiple_of((y ^ step) * size, size), size)
            out[at * size : (at + 1) * size, :] = keeps[at][rows, wide:] + others[at][rows, wide:]


def merge(place, keeps, others):
    rows, columns = keeps[0].shape
    out = jax.ShapeDtypeStruct((rows, columns // 2), jnp.float32)
    vmem = pl.BlockSpec(memory_space=pltpu.VMEM)
    outs = pl.pallas_call(
        merge_kernel,
        out_shape=[out] * 8,
        in_specs=[pl.BlockSpec(memory_space=pltpu.SMEM)] + [vmem] * 8,
        out_specs=[vmem] * 8,
        compiler_params=pltpu.CompilerParams(vmem_limit_bytes=32 * 2**20),
        cost_estimate=pl.CostEstimate(
            flops=2**20, bytes_accessed=12 * 2**20, transcendentals=0
        ),
        name="merge",
    )(place, *keeps, *others)
    return outs[:4], outs[4:]


def factor_steps(scale, first, last, tri_ref, inv_ref, work):
    n = work.shape[0]
    count = n // BLOCK
    for k in range(first, last):
        lo, hi = k * BLOCK, (k + 1) * BLOCK
        upper, inverse = factor_block(work[lo:hi, lo:hi])
        tri_ref[lo:hi, lo:hi] = upper * (1.0 / scale)
        if k:
            inv_ref[lo:hi, :lo] = dot(inverse, inv_ref[lo:hi, :lo])
        inv_ref[lo:hi, lo:hi] = inverse * scale
        if hi < n:
            panel = dot(inverse, work[lo:hi, hi:])
            tri_ref[lo:hi, hi:] = panel * (1.0 / scale)
            for i in range(k + 1, count):
                at = (i - k - 1) * BLOCK
                work[i * BLOCK : (i + 1) * BLOCK, i * BLOCK :] -= dot_first(
                    panel[:, at : at + BLOCK], panel[:, at:]
                )
            inv_ref[hi:, :hi] -= dot_first(panel, inv_ref[lo:hi, :hi])


def factor_first(scale, middle, place_ref, *refs):
    pieces, (tri_ref, inv_ref, work, packed) = refs[:8], refs[8:]
    piece = pieces[0].shape[0]
    core, y = place_ref[0], place_ref[1]
    for other in range(2):
        half = core if other == 0 else 1 - core
        for slot, step in enumerate((0,) + ORDER):
            start = (half * YS + (y ^ step)) * piece
            packed[pl.ds(pl.multiple_of(start, 8), piece), :] = pieces[other * 4 + slot][...]
    work[...] = jnp.zeros_like(work)
    for spot, (i, j) in enumerate(HALVES[0] + HALVES[1]):
        work[span(i), span(j)] = packed[span(spot), :]
    tri_ref[...] = jnp.zeros_like(tri_ref)
    inv_ref[...] = jnp.zeros_like(inv_ref)
    factor_steps(scale, 0, middle, tri_ref, inv_ref, work)


def factor_second(scale, middle, tri_in, inv_in, work_in, after, tri_ref, inv_ref, work):
    tri_ref[...] = tri_in[...]
    inv_ref[...] = inv_in[...]
    work[...] = work_in[...]
    factor_steps(scale, middle, work.shape[0] // BLOCK, tri_ref, inv_ref, work)


def factor_begin(place, pieces, n, scale, middle):
    whole = jax.ShapeDtypeStruct((n, n), jnp.float32)
    vmem = pl.BlockSpec(memory_space=pltpu.VMEM)
    return pl.pallas_call(
        functools.partial(factor_first, scale, middle),
        out_shape=(whole,) * 3,
        in_specs=[pl.BlockSpec(memory_space=pltpu.SMEM)] + [vmem] * 8,
        out_specs=(vmem,) * 3,
        scratch_shapes=[pltpu.VMEM((8 * pieces[0].shape[0], BLOCK), jnp.float32)],
        compiler_params=pltpu.CompilerParams(vmem_limit_bytes=32 * 2**20),
        cost_estimate=pl.CostEstimate(
            flops=12 * 10**9, bytes_accessed=4 * 2**20, transcendentals=0
        ),
        name="factor_begin",
    )(place, *pieces)


def factor_end(parts, after, n, scale, middle):
    whole = jax.ShapeDtypeStruct((n, n), jnp.float32)
    vmem = pl.BlockSpec(memory_space=pltpu.VMEM)
    return pl.pallas_call(
        functools.partial(factor_second, scale, middle),
        out_shape=(whole,) * 2,
        in_specs=[vmem] * 3 + [pl.BlockSpec(memory_space=pl.ANY)],
        out_specs=(vmem,) * 2,
        scratch_shapes=[pltpu.VMEM((n, n), jnp.float32)],
        compiler_params=pltpu.CompilerParams(vmem_limit_bytes=32 * 2**20),
        cost_estimate=pl.CostEstimate(
            flops=12 * 10**9, bytes_accessed=4 * 2**20, transcendentals=0
        ),
        name="factor_end",
    )(*parts, after)


def on_device(matrix, sketch):
    local_rows, width = matrix.shape
    shard, columns = sketch.shape
    total_rows = local_rows * lax.axis_size(("rows", "grp"))
    rows_place = lax.axis_index("rows")
    y = lax.axis_index("grp")
    core = lax.rem(rows_place, CORES)
    z = lax.rem(lax.div(rows_place, CORES), ZS)
    x = lax.div(rows_place, CORES * ZS)
    z_odd, z_pair = lax.rem(z, 2), lax.div(z, 2)
    place = jnp.stack([core, y, x]).astype(jnp.int32)
    tie = lax.optimization_barrier

    half = shard // CORES
    mine = cut(sketch, core, CORES, 0)
    arrived = [to_y(mine, step) for step in ORDER]
    passed = [to_core(value) for value in arrived]

    def part(start, value):
        strip = lax.dynamic_slice_in_dim(matrix, start, value.shape[0], axis=1)
        return jnp.dot(strip, value, preferred_element_type=jnp.float32)

    sketched = part(y * shard, sketch)
    for step, near, far in zip(ORDER, arrived, passed):
        source = (y ^ step) * shard
        sketched = sketched + part(source + core * half, near)
        sketched = sketched + part(source + (1 - core) * half, far)

    keep, send, stack = gram_pieces(place, sketched, (columns,))

    strips = []

    def strips_behind(count, *done):
        for _ in range(count):
            strips.append(product(place, stack, matrix, SEND[len(strips)]))
        tied, strips[-count:] = tie((done, strips[-count:]))
        return tied

    (other,) = strips_behind(2, to_core(send))
    summed = cut(keep, y, YS, 0) + cut(other, y, YS, 0)
    one, three, two = strips_behind(
        1,
        *[to_y(cut(keep, y ^ step, YS, 0) + cut(other, y ^ step, YS, 0), step) for step in ORDER],
    )
    summed = (summed + two) + (one + three)
    one, three, two = strips_behind(1, *[to_x(summed, step) for step in ORDER])
    summed = (summed + two) + (one + three)
    others = [to_core(sent) for _, sent in strips]
    summed = summed + to_z_pair(summed)
    summed, others = tie((summed, others))
    chunks_x, chunks_y = merge(place, [kept for kept, _ in strips], others)
    moved = [to_z(summed, step) for step in ORDER]
    (one, three, two), chunks_x, chunks_y = tie((moved, chunks_x, chunks_y))
    summed = (summed + two) + (one + three)
    pieces = [summed] + [to_y(summed, step) for step in ORDER]
    pieces = pieces + [to_core(value) for value in pieces]

    chunks_x, chunks_y, pieces = tie((chunks_x, chunks_y, pieces))
    moved_x = [to_x(chunk, step) for chunk, step in zip(chunks_x, ORDER)]
    moved_y = [to_y(chunk, step) for chunk, step in zip(chunks_y, ORDER)]
    root_rows = math.sqrt(total_rows)
    begun = factor_begin(place, pieces, columns, root_rows, 2)
    moved_y[:2], begun = tie((moved_y[:2], begun))
    triangle, inverse = factor_end(begun, moved_y[0], columns, root_rows, 2)
    moved_x, moved_y, _ = tie((moved_x, moved_y, inverse))
    over_x = chunks_x[3] + sum(moved_x)
    over_y = (chunks_y[3] + sum(moved_y)).reshape(XS, -1, columns // 2)
    over_x = scatter_sum(over_x, y, YS, to_y)
    over_y = over_y[3] + sum(to_x(over_y[at], step) for at, step in enumerate(ORDER))
    both = jnp.concatenate([over_x, over_y], axis=1)
    own = both.shape[0] // ZS
    both = both.reshape(ZS // 2, 2, own, columns)

    def parity(index):
        return lax.dynamic_index_in_dim(both, index, 1, keepdims=False)

    def through(value, precision):
        return lax.dot_general(
            value,
            inverse,
            (((1,), (1,)), ((), ())),
            precision=precision,
            preferred_element_type=jnp.float32,
        )

    basis_block = through(sketched, lax.Precision.HIGH).astype(jnp.bfloat16)
    other, basis_block = tie((to_z_pair(parity(1 - z_odd)), basis_block))
    both = parity(z_odd) + other
    strip = scatter_sum(both, z_pair, ZS // 2, to_z).reshape(own, columns)
    projected = through(strip, precise) * (math.sqrt(width) / total_rows)
    return (basis_block, triangle, projected)


def solution(mesh):
    return jax.shard_map(
        on_device,
        mesh=mesh,
        in_specs=(P(("rows", "grp"), None), P("grp", None)),
        out_specs=(P(("rows", "grp"), None), P(), P(("rows", "grp"), None)),
        check_vma=False,
    )
```

```python
import functools
import math

import jax
import jax.numpy as jnp
from jax import lax
from jax.experimental import pallas as pl
from jax.experimental.pallas import tpu as pltpu
from jax.sharding import PartitionSpec as P

precise = lax.Precision.HIGHEST
BLOCK = 128
TILE = 8
XS, ZS, CORES, YS = 4, 8, 2, 4


def row_pairs(move):
    pairs = []
    for x in range(XS):
        for z in range(ZS):
            for c in range(CORES):
                a, b, d = move(x, z, c)
                pairs.append(((x * ZS + z) * CORES + c, (a * ZS + b) * CORES + d))
    return pairs


def to_core(value):
    return lax.ppermute(value, "rows", row_pairs(lambda x, z, c: (x, z, 1 - c)))


def to_x(value, step):
    return lax.ppermute(value, "rows", row_pairs(lambda x, z, c: (x ^ step, z, c)))


def to_z(value, step):
    return lax.ppermute(value, "rows", row_pairs(lambda x, z, c: (x, z ^ (2 * step), c)))


def to_z_pair(value):
    return lax.ppermute(value, "rows", row_pairs(lambda x, z, c: (x, z ^ 1, c)))


def to_y(value, step):
    return lax.ppermute(value, "grp", [(y, y ^ step) for y in range(YS)])


ORDER = (1, 3, 2)


def cut(value, index, count, axis):
    size = value.shape[axis] // count
    return lax.dynamic_slice_in_dim(value, index * size, size, axis=axis)


def scatter_sum(value, place, count, send, axis=0):
    total = cut(value, place, count, axis)
    for step in ORDER:
        total = total + send(cut(value, place ^ step, count, axis), step)
    return total


def ring_sum(value, send):
    one, three, two = [send(value, step) for step in ORDER]
    return (value + two) + (one + three)


def lane_splat(tile, lane):
    return jnp.broadcast_to(tile[:, lane : lane + 1], tile.shape)


def row_splat(tile, row):
    return jnp.broadcast_to(tile[row : row + 1, :], tile.shape)


def factor_tile(own, base):
    columns = [lane_splat(own, base + j) for j in range(TILE)]
    a = [[row_splat(columns[j], i) if i >= j else None for j in range(TILE)] for i in range(TILE)]
    low = [[None] * TILE for _ in range(TILE)]
    inv = [None] * TILE
    for j in range(TILE):
        inv[j] = lax.rsqrt(a[j][j])
        for i in range(j + 1, TILE):
            low[i][j] = a[i][j] * inv[j]
        for i in range(j + 1, TILE):
            for k in range(j + 1, i + 1):
                a[i][k] = a[i][k] - low[i][j] * low[k][j]
    return low, inv


def forward(low, inv, values):
    solved = []
    for j in range(TILE):
        value = values[j]
        for m in range(j):
            value = value - low[j][m] * solved[m]
        solved.append(value * inv[j])
    return solved


def backward(low, inv, rows):
    solved = [None] * TILE
    for j in reversed(range(TILE)):
        value = rows[j]
        for m in range(TILE - 1, j, -1):
            value = value - low[m][j] * solved[m]
        solved[j] = value * inv[j]
    return solved


def factor_block(block):
    count = BLOCK // TILE
    row_id = lax.broadcasted_iota(jnp.int32, (TILE, BLOCK), 0)
    lane_id = lax.broadcasted_iota(jnp.int32, (TILE, BLOCK), 1)

    def merge_rows(rows):
        out = rows[0]
        for j in range(1, TILE):
            out = jnp.where(row_id == j, rows[j], out)
        return out

    left = [block[i * TILE : (i + 1) * TILE, :] for i in range(count)]
    right = [(lane_id == row_id + i * TILE).astype(jnp.float32) for i in range(count)]
    for t in range(count):
        low, inv = factor_tile(left[t], t * TILE)
        rows_left, rows_right = (
            forward(low, inv, [row_splat(tile[t], j) for j in range(TILE)])
            for tile in (left, right)
        )
        left[t], right[t] = merge_rows(rows_left), merge_rows(rows_right)
        if t + 1 < count:
            old = left[t + 1]
            factors = forward(low, inv, [lane_splat(old, t * TILE + j) for j in range(TILE)])
            for j in range(TILE):
                left[t + 1] = left[t + 1] - factors[j] * rows_left[j]
                right[t + 1] = right[t + 1] - factors[j] * rows_right[j]
        if t + 2 < count:
            back_left, back_right = backward(low, inv, rows_left), backward(low, inv, rows_right)
            for m in range(t + 2, count):
                old = left[m]
                for j in reversed(range(TILE)):
                    column = lane_splat(old, t * TILE + j)
                    left[m] = left[m] - column * back_left[j]
                    right[m] = right[m] - column * back_right[j]
    upper, inverse = jnp.concatenate(left, 0), jnp.concatenate(right, 0)
    row = lax.broadcasted_iota(jnp.int32, (BLOCK, BLOCK), 0)
    lane = lax.broadcasted_iota(jnp.int32, (BLOCK, BLOCK), 1)
    return jnp.where(lane >= row, upper, 0.0), inverse


def dot(a, b):
    return jnp.dot(a, b, precision=precise, preferred_element_type=jnp.float32)


def dot_first(a, b):
    return lax.dot_general(
        a, b, (((0,), (0,)), ((), ())), precision=precise, preferred_element_type=jnp.float32
    )


HALVES = (((0, 0), (0, 1), (0, 2), (0, 3), (3, 3)), ((1, 1), (1, 2), (1, 3), (2, 2), (2, 3)))


def span(index):
    return slice(index * BLOCK, (index + 1) * BLOCK)


def gram_kernel(place_ref, rows_ref, keep_ref, send_ref, *refs):
    stacks, packed = refs[:-1], refs[-1]
    core = place_ref[0]
    spot = 0
    for half in range(2):
        for i in sorted({i for i, _ in HALVES[half]}):
            lanes = [j for k, j in HALVES[half] if k == i]
            wide = slice(lanes[0] * BLOCK, (lanes[-1] + 1) * BLOCK)
            strip = dot_first(rows_ref[:, span(i)], rows_ref[:, wide])
            for at in range(len(lanes)):
                packed[span(spot), :] = strip[:, span(at)]
                spot += 1
    size = keep_ref.shape[0]
    keep_ref[...] = packed[pl.ds(pl.multiple_of(core * size, size), size), :]
    send_ref[...] = packed[pl.ds(pl.multiple_of((1 - core) * size, size), size), :]
    start = 0
    for stack_ref in stacks:
        wide = stack_ref.shape[0] // 2
        turned = rows_ref[:, start : start + wide].T
        high = turned.astype(jnp.bfloat16)
        stack_ref[:wide, :] = high
        stack_ref[wide:, :] = (turned - high.astype(jnp.float32)).astype(jnp.bfloat16)
        start += wide


def gram_pieces(place, sketched, widths):
    rows, columns = sketched.shape
    size = 5 * BLOCK
    vmem = pl.BlockSpec(memory_space=pltpu.VMEM)
    return pl.pallas_call(
        gram_kernel,
        out_shape=[jax.ShapeDtypeStruct((size, BLOCK), jnp.float32)] * 2
        + [jax.ShapeDtypeStruct((2 * wide, rows), jnp.bfloat16) for wide in widths],
        in_specs=[pl.BlockSpec(memory_space=pltpu.SMEM), vmem],
        out_specs=[vmem] * (2 + len(widths)),
        scratch_shapes=[pltpu.VMEM((2 * size, BLOCK), jnp.float32)],
        compiler_params=pltpu.CompilerParams(vmem_limit_bytes=40 * 2**20),
        cost_estimate=pl.CostEstimate(
            flops=2 * 10**9, bytes_accessed=8 * 2**20, transcendentals=0
        ),
        name="gram",
    )(place, sketched)


SEND = ORDER + (0,)


def product_kernel(own, place_ref, stack_ref, strip_ref, keep_ref, send_ref, held):
    core = place_ref[0]
    half = stack_ref.shape[0] // 2
    both = jnp.dot(stack_ref[...], strip_ref[...], preferred_element_type=jnp.float32)
    held[...] = (both[:half] + both[half:]).T
    for c in range(CORES):
        for wanted, out in ((core == c, keep_ref), (core != c, send_ref)):

            @pl.when(wanted)
            def _():
                for y in range(YS):
                    for z in range(ZS):
                        start = ((z * CORES + c) * YS + y) * own
                        spot = (y * ZS + z) * own
                        out[spot : spot + own, :] = held[start : start + own, :]


def product(place, stack, matrix, step):
    rows, width = matrix.shape
    wide = stack.shape[0] // 2
    strip = width // XS
    own = strip // (ZS * CORES * YS)
    out = pl.BlockSpec((strip // CORES, wide), lambda i, place_ref: (0, 0))
    return pl.pallas_call(
        functools.partial(product_kernel, own),
        grid_spec=pltpu.PrefetchScalarGridSpec(
            num_scalar_prefetch=1,
            grid=(1,),
            in_specs=[
                pl.BlockSpec(stack.shape, lambda i, place_ref: (0, 0)),
                pl.BlockSpec((rows, strip), lambda i, place_ref: (0, place_ref[2] ^ step)),
            ],
            out_specs=[out] * 2,
            scratch_shapes=[pltpu.VMEM((strip, wide), jnp.float32)],
        ),
        out_shape=[jax.ShapeDtypeStruct((strip // CORES, wide), jnp.float32)] * 2,
        compiler_params=pltpu.CompilerParams(vmem_limit_bytes=40 * 2**20),
        cost_estimate=pl.CostEstimate(
            flops=4 * rows * strip * wide, bytes_accessed=6 * 2**20, transcendentals=0
        ),
        name="product",
    )(place, stack, matrix)


def merge_kernel(place_ref, *refs):
    keeps, others, over_x, over_y = refs[:4], refs[4:8], refs[8:12], refs[12:16]
    y = place_ref[1]
    wide = over_x[0].shape[1]
    size = over_x[0].shape[0] // YS
    for at in range(XS):
        over_x[at][...] = keeps[at][:, :wide] + others[at][:, :wide]
        for out, step in zip(over_y, SEND):
            rows = pl.ds(pl.multiple_of((y ^ step) * size, size), size)
            out[at * size : (at + 1) * size, :] = keeps[at][rows, wide:] + others[at][rows, wide:]


def merge(place, keeps, others):
    rows, columns = keeps[0].shape
    out = pltpu.HBM((rows, columns // 2), jnp.float32)
    vmem = pl.BlockSpec(memory_space=pltpu.VMEM)
    outs = pl.pallas_call(
        merge_kernel,
        out_shape=[out] * 8,
        in_specs=[pl.BlockSpec(memory_space=pltpu.SMEM)] + [vmem] * 8,
        out_specs=[pl.BlockSpec((rows, columns // 2), lambda: (0, 0))] * 8,
        compiler_params=pltpu.CompilerParams(vmem_limit_bytes=16 * 2**20),
        cost_estimate=pl.CostEstimate(
            flops=2**20, bytes_accessed=12 * 2**20, transcendentals=0
        ),
        name="merge",
    )(place, *keeps, *others)
    return outs[:4], outs[4:]


def factor_steps(scale, first, last, tri_ref, inv_ref, work):
    n = work.shape[0]
    count = n // BLOCK
    for k in range(first, last):
        lo, hi = k * BLOCK, (k + 1) * BLOCK
        upper, inverse = factor_block(work[lo:hi, lo:hi])
        tri_ref[lo:hi, lo:hi] = upper * (1.0 / scale)
        if k:
            inv_ref[lo:hi, :lo] = dot(inverse, inv_ref[lo:hi, :lo])
        inv_ref[lo:hi, lo:hi] = inverse * scale
        if hi < n:
            panel = dot(inverse, work[lo:hi, hi:])
            tri_ref[lo:hi, hi:] = panel * (1.0 / scale)
            for i in range(k + 1, count):
                at = (i - k - 1) * BLOCK
                work[i * BLOCK : (i + 1) * BLOCK, i * BLOCK :] -= dot_first(
                    panel[:, at : at + BLOCK], panel[:, at:]
                )
            inv_ref[hi:, :hi] -= dot_first(panel, inv_ref[lo:hi, :hi])


def factor_first(scale, middle, place_ref, *refs):
    pieces, (tri_ref, inv_ref, work, packed) = refs[:8], refs[8:]
    piece = pieces[0].shape[0]
    core, y = place_ref[0], place_ref[1]
    for other in range(2):
        half = core if other == 0 else 1 - core
        for slot, step in enumerate((0,) + ORDER):
            start = (half * YS + (y ^ step)) * piece
            packed[pl.ds(pl.multiple_of(start, 8), piece), :] = pieces[other * 4 + slot][...]
    work[...] = jnp.zeros_like(work)
    for spot, (i, j) in enumerate(HALVES[0] + HALVES[1]):
        work[span(i), span(j)] = packed[span(spot), :]
    tri_ref[...] = jnp.zeros_like(tri_ref)
    inv_ref[...] = jnp.zeros_like(inv_ref)
    factor_steps(scale, 0, middle, tri_ref, inv_ref, work)


def factor_second(scale, middle, tri_in, inv_in, work_in, after, tri_ref, inv_ref, work):
    tri_ref[...] = tri_in[...]
    inv_ref[...] = inv_in[...]
    work[...] = work_in[...]
    factor_steps(scale, middle, work.shape[0] // BLOCK, tri_ref, inv_ref, work)


def factor_begin(place, pieces, n, scale, middle):
    whole = jax.ShapeDtypeStruct((n, n), jnp.float32)
    vmem = pl.BlockSpec(memory_space=pltpu.VMEM)
    return pl.pallas_call(
        functools.partial(factor_first, scale, middle),
        out_shape=(whole,) * 3,
        in_specs=[pl.BlockSpec(memory_space=pltpu.SMEM)] + [vmem] * 8,
        out_specs=(vmem,) * 3,
        scratch_shapes=[pltpu.VMEM((8 * pieces[0].shape[0], BLOCK), jnp.float32)],
        compiler_params=pltpu.CompilerParams(vmem_limit_bytes=12 * 2**20),
        cost_estimate=pl.CostEstimate(
            flops=12 * 10**9, bytes_accessed=4 * 2**20, transcendentals=0
        ),
        name="factor_begin",
    )(place, *pieces)


def factor_end(parts, after, n, scale, middle):
    whole = jax.ShapeDtypeStruct((n, n), jnp.float32)
    vmem = pl.BlockSpec(memory_space=pltpu.VMEM)
    return pl.pallas_call(
        functools.partial(factor_second, scale, middle),
        out_shape=(whole,) * 2,
        in_specs=[vmem] * 3 + [pl.BlockSpec(memory_space=pl.ANY)],
        out_specs=(vmem,) * 2,
        scratch_shapes=[pltpu.VMEM((n, n), jnp.float32)],
        compiler_params=pltpu.CompilerParams(vmem_limit_bytes=12 * 2**20),
        cost_estimate=pl.CostEstimate(
            flops=12 * 10**9, bytes_accessed=4 * 2**20, transcendentals=0
        ),
        name="factor_end",
    )(*parts, after)


def on_device(matrix, sketch):
    local_rows, width = matrix.shape
    shard, columns = sketch.shape
    total_rows = local_rows * lax.axis_size(("rows", "grp"))
    rows_place = lax.axis_index("rows")
    y = lax.axis_index("grp")
    core = lax.rem(rows_place, CORES)
    z = lax.rem(lax.div(rows_place, CORES), ZS)
    x = lax.div(rows_place, CORES * ZS)
    z_odd, z_pair = lax.rem(z, 2), lax.div(z, 2)
    place = jnp.stack([core, y, x]).astype(jnp.int32)
    tie = lax.optimization_barrier

    half = shard // CORES
    mine = cut(sketch, core, CORES, 0)
    arrived = [to_y(mine, step) for step in ORDER]
    passed = [to_core(value) for value in arrived]

    def part(start, value):
        strip = lax.dynamic_slice_in_dim(matrix, start, value.shape[0], axis=1)
        return jnp.dot(strip, value, preferred_element_type=jnp.float32)

    sketched = part(y * shard, sketch)
    for step, near, far in zip(ORDER, arrived, passed):
        source = (y ^ step) * shard
        sketched = sketched + part(source + core * half, near)
        sketched = sketched + part(source + (1 - core) * half, far)

    keep, send, stack = gram_pieces(place, sketched, (columns,))

    strips = []

    def strips_behind(count, *done):
        for _ in range(count):
            strips.append(product(place, stack, matrix, SEND[len(strips)]))
        tied, strips[-count:] = tie((done, strips[-count:]))
        return tied

    (other,) = strips_behind(2, to_core(send))
    summed = cut(keep, y, YS, 0) + cut(other, y, YS, 0)
    one, three, two = strips_behind(
        1,
        *[to_y(cut(keep, y ^ step, YS, 0) + cut(other, y ^ step, YS, 0), step) for step in ORDER],
    )
    summed = (summed + two) + (one + three)
    one, three, two = strips_behind(1, *[to_x(summed, step) for step in ORDER])
    summed = (summed + two) + (one + three)
    others = [to_core(sent) for _, sent in strips]
    summed = summed + to_z_pair(summed)
    summed, others = tie((summed, others))
    chunks_x, chunks_y = merge(place, [kept for kept, _ in strips], others)
    moved = [to_z(summed, step) for step in ORDER]
    (one, three, two), chunks_x, chunks_y = tie((moved, chunks_x, chunks_y))
    summed = (summed + two) + (one + three)
    pieces = [summed] + [to_y(summed, step) for step in ORDER]
    pieces = pieces + [to_core(value) for value in pieces]

    chunks_x, chunks_y, pieces = tie((chunks_x, chunks_y, pieces))
    moved_x = [to_x(chunk, step) for chunk, step in zip(chunks_x, ORDER)]
    moved_y = [to_y(chunk, step) for chunk, step in zip(chunks_y, ORDER)]
    root_rows = math.sqrt(total_rows)
    begun = factor_begin(place, pieces, columns, root_rows, 2)
    moved_y[:2], begun = tie((moved_y[:2], begun))
    triangle, inverse = factor_end(begun, moved_y[0], columns, root_rows, 2)
    moved_x, moved_y, _ = tie((moved_x, moved_y, inverse))
    over_x = chunks_x[3] + sum(moved_x)
    over_y = (chunks_y[3] + sum(moved_y)).reshape(XS, -1, columns // 2)
    over_x = scatter_sum(over_x, y, YS, to_y)
    over_y = over_y[3] + sum(to_x(over_y[at], step) for at, step in enumerate(ORDER))
    both = jnp.concatenate([over_x, over_y], axis=1)
    own = both.shape[0] // ZS
    both = both.reshape(ZS // 2, 2, own, columns)

    def parity(index):
        return lax.dynamic_index_in_dim(both, index, 1, keepdims=False)

    def through(value, precision):
        return lax.dot_general(
            value,
            inverse,
            (((1,), (1,)), ((), ())),
            precision=precision,
            preferred_element_type=jnp.float32,
        )

    basis_block = through(sketched, lax.Precision.HIGH).astype(jnp.bfloat16)
    other, basis_block = tie((to_z_pair(parity(1 - z_odd)), basis_block))
    both = parity(z_odd) + other
    strip = scatter_sum(both, z_pair, ZS // 2, to_z).reshape(own, columns)
    projected = through(strip, lax.Precision.HIGH) * (math.sqrt(width) / total_rows)
    return (basis_block, triangle, projected)


def solution(mesh):
    return jax.shard_map(
        on_device,
        mesh=mesh,
        in_specs=(P(("rows", "grp"), None), P("grp", None)),
        out_specs=(P(("rows", "grp"), None), P(), P(("rows", "grp"), None)),
        check_vma=False,
    )
```

```python
import functools
import math

import jax
import jax.numpy as jnp
from jax import lax
from jax.experimental import pallas as pl
from jax.experimental.pallas import tpu as pltpu
from jax.sharding import PartitionSpec as P

precise = lax.Precision.HIGHEST
BLOCK = 128
TILE = 8
XS, ZS, CORES, YS = 4, 8, 2, 4


def row_pairs(move):
    pairs = []
    for x in range(XS):
        for z in range(ZS):
            for c in range(CORES):
                a, b, d = move(x, z, c)
                pairs.append(((x * ZS + z) * CORES + c, (a * ZS + b) * CORES + d))
    return pairs


def to_core(value):
    return lax.ppermute(value, "rows", row_pairs(lambda x, z, c: (x, z, 1 - c)))


def to_x(value, step):
    return lax.ppermute(value, "rows", row_pairs(lambda x, z, c: (x ^ step, z, c)))


def to_z(value, step):
    return lax.ppermute(value, "rows", row_pairs(lambda x, z, c: (x, z ^ (2 * step), c)))


def to_z_pair(value):
    return lax.ppermute(value, "rows", row_pairs(lambda x, z, c: (x, z ^ 1, c)))


def to_y(value, step):
    return lax.ppermute(value, "grp", [(y, y ^ step) for y in range(YS)])


ORDER = (1, 3, 2)


def cut(value, index, count, axis):
    size = value.shape[axis] // count
    return lax.dynamic_slice_in_dim(value, index * size, size, axis=axis)


def scatter_sum(value, place, count, send, axis=0):
    total = cut(value, place, count, axis)
    for step in ORDER:
        total = total + send(cut(value, place ^ step, count, axis), step)
    return total


def ring_sum(value, send):
    one, three, two = [send(value, step) for step in ORDER]
    return (value + two) + (one + three)


def lane_splat(tile, lane):
    return jnp.broadcast_to(tile[:, lane : lane + 1], tile.shape)


def row_splat(tile, row):
    return jnp.broadcast_to(tile[row : row + 1, :], tile.shape)


def factor_tile(own, base):
    columns = [lane_splat(own, base + j) for j in range(TILE)]
    a = [[row_splat(columns[j], i) if i >= j else None for j in range(TILE)] for i in range(TILE)]
    low = [[None] * TILE for _ in range(TILE)]
    inv = [None] * TILE
    for j in range(TILE):
        inv[j] = lax.rsqrt(a[j][j])
        for i in range(j + 1, TILE):
            low[i][j] = a[i][j] * inv[j]
        for i in range(j + 1, TILE):
            for k in range(j + 1, i + 1):
                a[i][k] = a[i][k] - low[i][j] * low[k][j]
    return low, inv


def forward(low, inv, values):
    solved = []
    for j in range(TILE):
        value = values[j]
        for m in range(j):
            value = value - low[j][m] * solved[m]
        solved.append(value * inv[j])
    return solved


def backward(low, inv, rows):
    solved = [None] * TILE
    for j in reversed(range(TILE)):
        value = rows[j]
        for m in range(TILE - 1, j, -1):
            value = value - low[m][j] * solved[m]
        solved[j] = value * inv[j]
    return solved


def factor_block(block):
    count = BLOCK // TILE
    row_id = lax.broadcasted_iota(jnp.int32, (TILE, BLOCK), 0)
    lane_id = lax.broadcasted_iota(jnp.int32, (TILE, BLOCK), 1)

    def merge_rows(rows):
        out = rows[0]
        for j in range(1, TILE):
            out = jnp.where(row_id == j, rows[j], out)
        return out

    left = [block[i * TILE : (i + 1) * TILE, :] for i in range(count)]
    right = [(lane_id == row_id + i * TILE).astype(jnp.float32) for i in range(count)]
    for t in range(count):
        low, inv = factor_tile(left[t], t * TILE)
        rows_left, rows_right = (
            forward(low, inv, [row_splat(tile[t], j) for j in range(TILE)])
            for tile in (left, right)
        )
        left[t], right[t] = merge_rows(rows_left), merge_rows(rows_right)
        if t + 1 < count:
            old = left[t + 1]
            factors = forward(low, inv, [lane_splat(old, t * TILE + j) for j in range(TILE)])
            for j in range(TILE):
                left[t + 1] = left[t + 1] - factors[j] * rows_left[j]
                right[t + 1] = right[t + 1] - factors[j] * rows_right[j]
        if t + 2 < count:
            back_left, back_right = backward(low, inv, rows_left), backward(low, inv, rows_right)
            for m in range(t + 2, count):
                old = left[m]
                for j in reversed(range(TILE)):
                    column = lane_splat(old, t * TILE + j)
                    left[m] = left[m] - column * back_left[j]
                    right[m] = right[m] - column * back_right[j]
    upper, inverse = jnp.concatenate(left, 0), jnp.concatenate(right, 0)
    row = lax.broadcasted_iota(jnp.int32, (BLOCK, BLOCK), 0)
    lane = lax.broadcasted_iota(jnp.int32, (BLOCK, BLOCK), 1)
    return jnp.where(lane >= row, upper, 0.0), inverse


def dot(a, b):
    return jnp.dot(a, b, precision=precise, preferred_element_type=jnp.float32)


def dot_first(a, b):
    return lax.dot_general(
        a, b, (((0,), (0,)), ((), ())), precision=precise, preferred_element_type=jnp.float32
    )


HALVES = (((0, 0), (0, 1), (0, 2), (0, 3), (3, 3)), ((1, 1), (1, 2), (1, 3), (2, 2), (2, 3)))


def span(index):
    return slice(index * BLOCK, (index + 1) * BLOCK)


def gram_kernel(place_ref, rows_ref, keep_ref, send_ref, *refs):
    stacks, packed = refs[:-1], refs[-1]
    core = place_ref[0]
    spot = 0
    for half in range(2):
        for i in sorted({i for i, _ in HALVES[half]}):
            lanes = [j for k, j in HALVES[half] if k == i]
            wide = slice(lanes[0] * BLOCK, (lanes[-1] + 1) * BLOCK)
            strip = dot_first(rows_ref[:, span(i)], rows_ref[:, wide])
            for at in range(len(lanes)):
                packed[span(spot), :] = strip[:, span(at)]
                spot += 1
    size = keep_ref.shape[0]
    keep_ref[...] = packed[pl.ds(pl.multiple_of(core * size, size), size), :]
    send_ref[...] = packed[pl.ds(pl.multiple_of((1 - core) * size, size), size), :]
    start = 0
    for stack_ref in stacks:
        wide = stack_ref.shape[0] // 2
        turned = rows_ref[:, start : start + wide].T
        high = turned.astype(jnp.bfloat16)
        stack_ref[:wide, :] = high
        stack_ref[wide:, :] = (turned - high.astype(jnp.float32)).astype(jnp.bfloat16)
        start += wide


def gram_pieces(place, sketched, widths):
    rows, columns = sketched.shape
    size = 5 * BLOCK
    vmem = pl.BlockSpec(memory_space=pltpu.VMEM)
    return pl.pallas_call(
        gram_kernel,
        out_shape=[jax.ShapeDtypeStruct((size, BLOCK), jnp.float32)] * 2
        + [jax.ShapeDtypeStruct((2 * wide, rows), jnp.bfloat16) for wide in widths],
        in_specs=[pl.BlockSpec(memory_space=pltpu.SMEM), vmem],
        out_specs=[vmem] * (2 + len(widths)),
        scratch_shapes=[pltpu.VMEM((2 * size, BLOCK), jnp.float32)],
        compiler_params=pltpu.CompilerParams(vmem_limit_bytes=40 * 2**20),
        cost_estimate=pl.CostEstimate(
            flops=2 * 10**9, bytes_accessed=8 * 2**20, transcendentals=0
        ),
        name="gram",
    )(place, sketched)


SEND = ORDER + (0,)


def product_kernel(own, place_ref, stack_ref, strip_ref, keep_ref, send_ref, held):
    core = place_ref[0]
    half = stack_ref.shape[0] // 2
    both = jnp.dot(stack_ref[...], strip_ref[...], preferred_element_type=jnp.float32)
    held[...] = (both[:half] + both[half:]).T
    for c in range(CORES):
        for wanted, out in ((core == c, keep_ref), (core != c, send_ref)):

            @pl.when(wanted)
            def _():
                for y in range(YS):
                    for z in range(ZS):
                        start = ((z * CORES + c) * YS + y) * own
                        spot = (y * ZS + z) * own
                        out[spot : spot + own, :] = held[start : start + own, :]


def product(place, stack, matrix, step):
    rows, width = matrix.shape
    wide = stack.shape[0] // 2
    strip = width // XS
    own = strip // (ZS * CORES * YS)
    out = pl.BlockSpec((strip // CORES, wide), lambda i, place_ref: (0, 0))
    return pl.pallas_call(
        functools.partial(product_kernel, own),
        grid_spec=pltpu.PrefetchScalarGridSpec(
            num_scalar_prefetch=1,
            grid=(1,),
            in_specs=[
                pl.BlockSpec(stack.shape, lambda i, place_ref: (0, 0)),
                pl.BlockSpec((rows, strip), lambda i, place_ref: (0, place_ref[2] ^ step)),
            ],
            out_specs=[out] * 2,
            scratch_shapes=[pltpu.VMEM((strip, wide), jnp.float32)],
        ),
        out_shape=[jax.ShapeDtypeStruct((strip // CORES, wide), jnp.float32)] * 2,
        compiler_params=pltpu.CompilerParams(vmem_limit_bytes=40 * 2**20),
        cost_estimate=pl.CostEstimate(
            flops=4 * rows * strip * wide, bytes_accessed=6 * 2**20, transcendentals=0
        ),
        name="product",
    )(place, stack, matrix)


def merge_kernel(place_ref, *refs):
    keeps, others, over_x, over_y = refs[:4], refs[4:8], refs[8:12], refs[12:16]
    y = place_ref[1]
    wide = over_x[0].shape[1]
    size = over_x[0].shape[0] // YS
    for at in range(XS):
        over_x[at][...] = keeps[at][:, :wide] + others[at][:, :wide]
        for out, step in zip(over_y, SEND):
            rows = pl.ds(pl.multiple_of((y ^ step) * size, size), size)
            out[at * size : (at + 1) * size, :] = keeps[at][rows, wide:] + others[at][rows, wide:]


def merge(place, keeps, others):
    rows, columns = keeps[0].shape
    out = pltpu.HBM((rows, columns // 2), jnp.float32)
    vmem = pl.BlockSpec(memory_space=pltpu.VMEM)
    outs = pl.pallas_call(
        merge_kernel,
        out_shape=[out] * 8,
        in_specs=[pl.BlockSpec(memory_space=pltpu.SMEM)] + [vmem] * 8,
        out_specs=[pl.BlockSpec((rows, columns // 2), lambda: (0, 0))] * 8,
        compiler_params=pltpu.CompilerParams(vmem_limit_bytes=16 * 2**20),
        cost_estimate=pl.CostEstimate(
            flops=2**20, bytes_accessed=12 * 2**20, transcendentals=0
        ),
        name="merge",
    )(place, *keeps, *others)
    return list(outs[:4]), list(outs[4:])


def factor_steps(scale, first, last, tri_ref, inv_ref, work):
    n = work.shape[0]
    count = n // BLOCK
    for k in range(first, last):
        lo, hi = k * BLOCK, (k + 1) * BLOCK
        upper, inverse = factor_block(work[lo:hi, lo:hi])
        tri_ref[lo:hi, lo:hi] = upper * (1.0 / scale)
        if k:
            inv_ref[lo:hi, :lo] = dot(inverse, inv_ref[lo:hi, :lo])
        inv_ref[lo:hi, lo:hi] = inverse * scale
        if hi < n:
            panel = dot(inverse, work[lo:hi, hi:])
            tri_ref[lo:hi, hi:] = panel * (1.0 / scale)
            for i in range(k + 1, count):
                at = (i - k - 1) * BLOCK
                work[i * BLOCK : (i + 1) * BLOCK, i * BLOCK :] -= dot_first(
                    panel[:, at : at + BLOCK], panel[:, at:]
                )
            inv_ref[hi:, :hi] -= dot_first(panel, inv_ref[lo:hi, :hi])


def factor_first(scale, middle, place_ref, *refs):
    pieces, (tri_ref, inv_ref, work, packed) = refs[:8], refs[8:]
    piece = pieces[0].shape[0]
    core, y = place_ref[0], place_ref[1]
    for other in range(2):
        half = core if other == 0 else 1 - core
        for slot, step in enumerate((0,) + ORDER):
            start = (half * YS + (y ^ step)) * piece
            packed[pl.ds(pl.multiple_of(start, 8), piece), :] = pieces[other * 4 + slot][...]
    work[...] = jnp.zeros_like(work)
    for spot, (i, j) in enumerate(HALVES[0] + HALVES[1]):
        work[span(i), span(j)] = packed[span(spot), :]
    tri_ref[...] = jnp.zeros_like(tri_ref)
    inv_ref[...] = jnp.zeros_like(inv_ref)
    factor_steps(scale, 0, middle, tri_ref, inv_ref, work)


def factor_second(scale, middle, tri_in, inv_in, work_in, after, tri_ref, inv_ref, work):
    tri_ref[...] = tri_in[...]
    inv_ref[...] = inv_in[...]
    work[...] = work_in[...]
    factor_steps(scale, middle, work.shape[0] // BLOCK, tri_ref, inv_ref, work)


def factor_begin(place, pieces, n, scale, middle):
    whole = jax.ShapeDtypeStruct((n, n), jnp.float32)
    vmem = pl.BlockSpec(memory_space=pltpu.VMEM)
    return pl.pallas_call(
        functools.partial(factor_first, scale, middle),
        out_shape=(whole,) * 3,
        in_specs=[pl.BlockSpec(memory_space=pltpu.SMEM)] + [vmem] * 8,
        out_specs=(vmem,) * 3,
        scratch_shapes=[pltpu.VMEM((8 * pieces[0].shape[0], BLOCK), jnp.float32)],
        compiler_params=pltpu.CompilerParams(vmem_limit_bytes=12 * 2**20),
        cost_estimate=pl.CostEstimate(
            flops=12 * 10**9, bytes_accessed=4 * 2**20, transcendentals=0
        ),
        name="factor_begin",
    )(place, *pieces)


def factor_end(parts, after, n, scale, middle):
    whole = jax.ShapeDtypeStruct((n, n), jnp.float32)
    vmem = pl.BlockSpec(memory_space=pltpu.VMEM)
    return pl.pallas_call(
        functools.partial(factor_second, scale, middle),
        out_shape=(whole,) * 2,
        in_specs=[vmem] * 3 + [pl.BlockSpec(memory_space=pl.ANY)],
        out_specs=(vmem,) * 2,
        scratch_shapes=[pltpu.VMEM((n, n), jnp.float32)],
        compiler_params=pltpu.CompilerParams(vmem_limit_bytes=12 * 2**20),
        cost_estimate=pl.CostEstimate(
            flops=12 * 10**9, bytes_accessed=4 * 2**20, transcendentals=0
        ),
        name="factor_end",
    )(*parts, after)


def on_device(matrix, sketch):
    local_rows, width = matrix.shape
    shard, columns = sketch.shape
    total_rows = local_rows * lax.axis_size(("rows", "grp"))
    rows_place = lax.axis_index("rows")
    y = lax.axis_index("grp")
    core = lax.rem(rows_place, CORES)
    z = lax.rem(lax.div(rows_place, CORES), ZS)
    x = lax.div(rows_place, CORES * ZS)
    z_odd, z_pair = lax.rem(z, 2), lax.div(z, 2)
    place = jnp.stack([core, y, x]).astype(jnp.int32)
    tie = lax.optimization_barrier

    half = shard // CORES
    mine = cut(sketch, core, CORES, 0)
    arrived = [to_y(mine, step) for step in ORDER]
    passed = [to_core(value) for value in arrived]

    def part(start, value):
        strip = lax.dynamic_slice_in_dim(matrix, start, value.shape[0], axis=1)
        return jnp.dot(strip, value, preferred_element_type=jnp.float32)

    sketched = part(y * shard, sketch)
    for step, near, far in zip(ORDER, arrived, passed):
        source = (y ^ step) * shard
        sketched = sketched + part(source + core * half, near)
        sketched = sketched + part(source + (1 - core) * half, far)

    keep, send, stack = gram_pieces(place, sketched, (columns,))

    strips = []

    def strips_behind(count, *done):
        for _ in range(count):
            strips.append(product(place, stack, matrix, SEND[len(strips)]))
        tied, strips[-count:] = tie((done, strips[-count:]))
        return tied

    (other,) = strips_behind(2, to_core(send))
    summed = cut(keep, y, YS, 0) + cut(other, y, YS, 0)
    one, three, two = strips_behind(
        1,
        *[to_y(cut(keep, y ^ step, YS, 0) + cut(other, y ^ step, YS, 0), step) for step in ORDER],
    )
    summed = (summed + two) + (one + three)
    one, three, two = strips_behind(1, *[to_x(summed, step) for step in ORDER])
    summed = (summed + two) + (one + three)
    others = [to_core(sent) for _, sent in strips]
    summed = summed + to_z_pair(summed)
    summed, others = tie((summed, others))
    chunks_x, chunks_y = merge(place, [kept for kept, _ in strips], others)
    moved = [to_z(summed, step) for step in ORDER]
    (one, three, two), chunks_x, chunks_y = tie((moved, chunks_x, chunks_y))
    chunks_x = list(chunks_x)
    summed = (summed + two) + (one + three)
    pieces = [summed] + [to_y(summed, step) for step in ORDER]
    pieces = pieces + [to_core(value) for value in pieces]

    chunks_x[2:], chunks_y, pieces = tie((chunks_x[2:], chunks_y, pieces))
    moved_x = [to_x(chunk, step) for chunk, step in zip(chunks_x, ORDER)]
    moved_y = [to_y(chunk, step) for chunk, step in zip(chunks_y, ORDER)]
    root_rows = math.sqrt(total_rows)
    begun = factor_begin(place, pieces, columns, root_rows, 2)
    moved_y[:2], begun = tie((moved_y[:2], begun))
    triangle, inverse = factor_end(begun, moved_y[0], columns, root_rows, 2)
    moved_x, moved_y, _ = tie((moved_x, moved_y, inverse))
    over_x = chunks_x[3] + sum(moved_x)
    over_y = (chunks_y[3] + sum(moved_y)).reshape(XS, -1, columns // 2)
    over_x = scatter_sum(over_x, y, YS, to_y)
    over_y = over_y[3] + sum(to_x(over_y[at], step) for at, step in enumerate(ORDER))
    both = jnp.concatenate([over_x, over_y], axis=1)
    own = both.shape[0] // ZS
    both = both.reshape(ZS // 2, 2, own, columns)

    def parity(index):
        return lax.dynamic_index_in_dim(both, index, 1, keepdims=False)

    def through(value, precision):
        return lax.dot_general(
            value,
            inverse,
            (((1,), (1,)), ((), ())),
            precision=precision,
            preferred_element_type=jnp.float32,
        )

    basis_block = through(sketched, lax.Precision.HIGH).astype(jnp.bfloat16)
    other, basis_block = tie((to_z_pair(parity(1 - z_odd)), basis_block))
    both = parity(z_odd) + other
    strip = scatter_sum(both, z_pair, ZS // 2, to_z).reshape(own, columns)
    projected = through(strip, lax.Precision.HIGH) * (math.sqrt(width) / total_rows)
    return (basis_block, triangle, projected)


def solution(mesh):
    return jax.shard_map(
        on_device,
        mesh=mesh,
        in_specs=(P(("rows", "grp"), None), P("grp", None)),
        out_specs=(P(("rows", "grp"), None), P(), P(("rows", "grp"), None)),
        check_vma=False,
    )
```

```python
import functools
import math

import jax
import jax.numpy as jnp
from jax import lax
from jax.experimental import pallas as pl
from jax.experimental.pallas import tpu as pltpu
from jax.sharding import PartitionSpec as P

precise = lax.Precision.HIGHEST
BLOCK = 128
TILE = 8
XS, ZS, CORES, YS = 4, 8, 2, 4


def row_pairs(move):
    pairs = []
    for x in range(XS):
        for z in range(ZS):
            for c in range(CORES):
                a, b, d = move(x, z, c)
                pairs.append(((x * ZS + z) * CORES + c, (a * ZS + b) * CORES + d))
    return pairs


def to_core(value):
    return lax.ppermute(value, "rows", row_pairs(lambda x, z, c: (x, z, 1 - c)))


def to_x(value, step):
    return lax.ppermute(value, "rows", row_pairs(lambda x, z, c: (x ^ step, z, c)))


def to_z(value, step):
    return lax.ppermute(value, "rows", row_pairs(lambda x, z, c: (x, z ^ (2 * step), c)))


def to_z_pair(value):
    return lax.ppermute(value, "rows", row_pairs(lambda x, z, c: (x, z ^ 1, c)))


def to_y(value, step):
    return lax.ppermute(value, "grp", [(y, y ^ step) for y in range(YS)])


ORDER = (1, 3, 2)
FAR_FIRST = (2, 1, 3)


def cut(value, index, count, axis):
    size = value.shape[axis] // count
    return lax.dynamic_slice_in_dim(value, index * size, size, axis=axis)


def scatter_sum(value, place, count, send, axis=0, order=ORDER):
    total = cut(value, place, count, axis)
    for step in order:
        total = total + send(cut(value, place ^ step, count, axis), step)
    return total


def ring_sum(value, send):
    one, three, two = [send(value, step) for step in ORDER]
    return (value + two) + (one + three)


def lane_splat(tile, lane):
    return jnp.broadcast_to(tile[:, lane : lane + 1], tile.shape)


def row_splat(tile, row):
    return jnp.broadcast_to(tile[row : row + 1, :], tile.shape)


def factor_tile(own, base):
    columns = [lane_splat(own, base + j) for j in range(TILE)]
    a = [[row_splat(columns[j], i) if i >= j else None for j in range(TILE)] for i in range(TILE)]
    low = [[None] * TILE for _ in range(TILE)]
    inv = [None] * TILE
    for j in range(TILE):
        inv[j] = lax.rsqrt(a[j][j])
        for i in range(j + 1, TILE):
            low[i][j] = a[i][j] * inv[j]
        for i in range(j + 1, TILE):
            for k in range(j + 1, i + 1):
                a[i][k] = a[i][k] - low[i][j] * low[k][j]
    return low, inv


def forward(low, inv, values):
    solved = []
    for j in range(TILE):
        value = values[j]
        for m in range(j):
            value = value - low[j][m] * solved[m]
        solved.append(value * inv[j])
    return solved


def backward(low, inv, rows):
    solved = [None] * TILE
    for j in reversed(range(TILE)):
        value = rows[j]
        for m in range(TILE - 1, j, -1):
            value = value - low[m][j] * solved[m]
        solved[j] = value * inv[j]
    return solved


def factor_block(block):
    count = BLOCK // TILE
    row_id = lax.broadcasted_iota(jnp.int32, (TILE, BLOCK), 0)
    lane_id = lax.broadcasted_iota(jnp.int32, (TILE, BLOCK), 1)

    def merge_rows(rows):
        out = rows[0]
        for j in range(1, TILE):
            out = jnp.where(row_id == j, rows[j], out)
        return out

    left = [block[i * TILE : (i + 1) * TILE, :] for i in range(count)]
    right = [(lane_id == row_id + i * TILE).astype(jnp.float32) for i in range(count)]
    for t in range(count):
        low, inv = factor_tile(left[t], t * TILE)
        rows_left, rows_right = (
            forward(low, inv, [row_splat(tile[t], j) for j in range(TILE)])
            for tile in (left, right)
        )
        left[t], right[t] = merge_rows(rows_left), merge_rows(rows_right)
        if t + 1 < count:
            old = left[t + 1]
            factors = forward(low, inv, [lane_splat(old, t * TILE + j) for j in range(TILE)])
            for j in range(TILE):
                left[t + 1] = left[t + 1] - factors[j] * rows_left[j]
                right[t + 1] = right[t + 1] - factors[j] * rows_right[j]
        if t + 2 < count:
            back_left, back_right = backward(low, inv, rows_left), backward(low, inv, rows_right)
            for m in range(t + 2, count):
                old = left[m]
                for j in reversed(range(TILE)):
                    column = lane_splat(old, t * TILE + j)
                    left[m] = left[m] - column * back_left[j]
                    right[m] = right[m] - column * back_right[j]
    upper, inverse = jnp.concatenate(left, 0), jnp.concatenate(right, 0)
    row = lax.broadcasted_iota(jnp.int32, (BLOCK, BLOCK), 0)
    lane = lax.broadcasted_iota(jnp.int32, (BLOCK, BLOCK), 1)
    return jnp.where(lane >= row, upper, 0.0), inverse


def dot(a, b):
    return jnp.dot(a, b, precision=precise, preferred_element_type=jnp.float32)


def dot_first(a, b):
    return lax.dot_general(
        a, b, (((0,), (0,)), ((), ())), precision=precise, preferred_element_type=jnp.float32
    )


HALVES = (((0, 0), (0, 1), (0, 2), (0, 3), (3, 3)), ((1, 1), (1, 2), (1, 3), (2, 2), (2, 3)))


def span(index):
    return slice(index * BLOCK, (index + 1) * BLOCK)


def gram_kernel(place_ref, rows_ref, keep_ref, send_ref, *refs):
    stacks, packed = refs[:-1], refs[-1]
    core = place_ref[0]
    spot = 0
    for half in range(2):
        for i in sorted({i for i, _ in HALVES[half]}):
            lanes = [j for k, j in HALVES[half] if k == i]
            wide = slice(lanes[0] * BLOCK, (lanes[-1] + 1) * BLOCK)
            strip = dot_first(rows_ref[:, span(i)], rows_ref[:, wide])
            for at in range(len(lanes)):
                packed[span(spot), :] = strip[:, span(at)]
                spot += 1
    size = keep_ref.shape[0]
    keep_ref[...] = packed[pl.ds(pl.multiple_of(core * size, size), size), :]
    send_ref[...] = packed[pl.ds(pl.multiple_of((1 - core) * size, size), size), :]
    start = 0
    for stack_ref in stacks:
        wide = stack_ref.shape[0] // 2
        turned = rows_ref[:, start : start + wide].T
        high = turned.astype(jnp.bfloat16)
        stack_ref[:wide, :] = high
        stack_ref[wide:, :] = (turned - high.astype(jnp.float32)).astype(jnp.bfloat16)
        start += wide


def gram_pieces(place, sketched, widths):
    rows, columns = sketched.shape
    size = 5 * BLOCK
    vmem = pl.BlockSpec(memory_space=pltpu.VMEM)
    return pl.pallas_call(
        gram_kernel,
        out_shape=[jax.ShapeDtypeStruct((size, BLOCK), jnp.float32)] * 2
        + [jax.ShapeDtypeStruct((2 * wide, rows), jnp.bfloat16) for wide in widths],
        in_specs=[pl.BlockSpec(memory_space=pltpu.SMEM), vmem],
        out_specs=[vmem] * (2 + len(widths)),
        scratch_shapes=[pltpu.VMEM((2 * size, BLOCK), jnp.float32)],
        compiler_params=pltpu.CompilerParams(vmem_limit_bytes=40 * 2**20),
        cost_estimate=pl.CostEstimate(
            flops=2 * 10**9, bytes_accessed=8 * 2**20, transcendentals=0
        ),
        name="gram",
    )(place, sketched)


SEND = ORDER + (0,)


def product_kernel(own, place_ref, stack_ref, strip_ref, keep_ref, send_ref, held):
    core = place_ref[0]
    half = stack_ref.shape[0] // 2
    both = jnp.dot(stack_ref[...], strip_ref[...], preferred_element_type=jnp.float32)
    held[...] = (both[:half] + both[half:]).T
    for c in range(CORES):
        for wanted, out in ((core == c, keep_ref), (core != c, send_ref)):

            @pl.when(wanted)
            def _():
                for y in range(YS):
                    for z in range(ZS):
                        start = ((z * CORES + c) * YS + y) * own
                        spot = (y * ZS + z) * own
                        out[spot : spot + own, :] = held[start : start + own, :]


def product(place, stack, matrix, step):
    rows, width = matrix.shape
    wide = stack.shape[0] // 2
    strip = width // XS
    own = strip // (ZS * CORES * YS)
    out = pl.BlockSpec((strip // CORES, wide), lambda i, place_ref: (0, 0))
    return pl.pallas_call(
        functools.partial(product_kernel, own),
        grid_spec=pltpu.PrefetchScalarGridSpec(
            num_scalar_prefetch=1,
            grid=(1,),
            in_specs=[
                pl.BlockSpec(stack.shape, lambda i, place_ref: (0, 0)),
                pl.BlockSpec((rows, strip), lambda i, place_ref: (0, place_ref[2] ^ step)),
            ],
            out_specs=[out] * 2,
            scratch_shapes=[pltpu.VMEM((strip, wide), jnp.float32)],
        ),
        out_shape=[jax.ShapeDtypeStruct((strip // CORES, wide), jnp.float32)] * 2,
        compiler_params=pltpu.CompilerParams(vmem_limit_bytes=40 * 2**20),
        cost_estimate=pl.CostEstimate(
            flops=4 * rows * strip * wide, bytes_accessed=6 * 2**20, transcendentals=0
        ),
        name="product",
    )(place, stack, matrix)


def merge_kernel(place_ref, *refs):
    keeps, others, over_x, over_y = refs[:4], refs[4:8], refs[8:12], refs[12:16]
    y = place_ref[1]
    wide = over_x[0].shape[1]
    size = over_x[0].shape[0] // YS
    for at in range(XS):
        over_x[at][...] = keeps[at][:, :wide] + others[at][:, :wide]
        for out, step in zip(over_y, SEND):
            rows = pl.ds(pl.multiple_of((y ^ step) * size, size), size)
            out[at * size : (at + 1) * size, :] = keeps[at][rows, wide:] + others[at][rows, wide:]


def merge(place, keeps, others):
    rows, columns = keeps[0].shape
    out = pltpu.HBM((rows, columns // 2), jnp.float32)
    vmem = pl.BlockSpec(memory_space=pltpu.VMEM)
    outs = pl.pallas_call(
        merge_kernel,
        out_shape=[out] * 8,
        in_specs=[pl.BlockSpec(memory_space=pltpu.SMEM)] + [vmem] * 8,
        out_specs=[pl.BlockSpec((rows, columns // 2), lambda: (0, 0))] * 8,
        compiler_params=pltpu.CompilerParams(vmem_limit_bytes=16 * 2**20),
        cost_estimate=pl.CostEstimate(
            flops=2**20, bytes_accessed=12 * 2**20, transcendentals=0
        ),
        name="merge",
    )(place, *keeps, *others)
    return list(outs[:4]), list(outs[4:])


def factor_steps(scale, first, last, tri_ref, inv_ref, work):
    n = work.shape[0]
    count = n // BLOCK
    for k in range(first, last):
        lo, hi = k * BLOCK, (k + 1) * BLOCK
        upper, inverse = factor_block(work[lo:hi, lo:hi])
        tri_ref[lo:hi, lo:hi] = upper * (1.0 / scale)
        if k:
            inv_ref[lo:hi, :lo] = dot(inverse, inv_ref[lo:hi, :lo])
        inv_ref[lo:hi, lo:hi] = inverse * scale
        if hi < n:
            panel = dot(inverse, work[lo:hi, hi:])
            tri_ref[lo:hi, hi:] = panel * (1.0 / scale)
            for i in range(k + 1, count):
                at = (i - k - 1) * BLOCK
                work[i * BLOCK : (i + 1) * BLOCK, i * BLOCK :] -= dot_first(
                    panel[:, at : at + BLOCK], panel[:, at:]
                )
            inv_ref[hi:, :hi] -= dot_first(panel, inv_ref[lo:hi, :hi])


def factor_first(scale, middle, place_ref, *refs):
    pieces, (tri_ref, inv_ref, work, packed) = refs[:8], refs[8:]
    piece = pieces[0].shape[0]
    core, y = place_ref[0], place_ref[1]
    for other in range(2):
        half = core if other == 0 else 1 - core
        for slot, step in enumerate((0,) + ORDER):
            start = (half * YS + (y ^ step)) * piece
            packed[pl.ds(pl.multiple_of(start, 8), piece), :] = pieces[other * 4 + slot][...]
    work[...] = jnp.zeros_like(work)
    for spot, (i, j) in enumerate(HALVES[0] + HALVES[1]):
        work[span(i), span(j)] = packed[span(spot), :]
    tri_ref[...] = jnp.zeros_like(tri_ref)
    inv_ref[...] = jnp.zeros_like(inv_ref)
    factor_steps(scale, 0, middle, tri_ref, inv_ref, work)


def factor_second(scale, middle, tri_in, inv_in, work_in, after, tri_ref, inv_ref, work):
    tri_ref[...] = tri_in[...]
    inv_ref[...] = inv_in[...]
    work[...] = work_in[...]
    factor_steps(scale, middle, work.shape[0] // BLOCK, tri_ref, inv_ref, work)


def factor_begin(place, pieces, n, scale, middle):
    whole = jax.ShapeDtypeStruct((n, n), jnp.float32)
    vmem = pl.BlockSpec(memory_space=pltpu.VMEM)
    return pl.pallas_call(
        functools.partial(factor_first, scale, middle),
        out_shape=(whole,) * 3,
        in_specs=[pl.BlockSpec(memory_space=pltpu.SMEM)] + [vmem] * 8,
        out_specs=(vmem,) * 3,
        scratch_shapes=[pltpu.VMEM((8 * pieces[0].shape[0], BLOCK), jnp.float32)],
        compiler_params=pltpu.CompilerParams(vmem_limit_bytes=12 * 2**20),
        cost_estimate=pl.CostEstimate(
            flops=12 * 10**9, bytes_accessed=4 * 2**20, transcendentals=0
        ),
        name="factor_begin",
    )(place, *pieces)


def factor_end(parts, after, n, scale, middle):
    whole = jax.ShapeDtypeStruct((n, n), jnp.float32)
    vmem = pl.BlockSpec(memory_space=pltpu.VMEM)
    return pl.pallas_call(
        functools.partial(factor_second, scale, middle),
        out_shape=(whole,) * 2,
        in_specs=[vmem] * 3 + [pl.BlockSpec(memory_space=pl.ANY)],
        out_specs=(vmem,) * 2,
        scratch_shapes=[pltpu.VMEM((n, n), jnp.float32)],
        compiler_params=pltpu.CompilerParams(vmem_limit_bytes=12 * 2**20),
        cost_estimate=pl.CostEstimate(
            flops=12 * 10**9, bytes_accessed=4 * 2**20, transcendentals=0
        ),
        name="factor_end",
    )(*parts, after)


def on_device(matrix, sketch):
    local_rows, width = matrix.shape
    shard, columns = sketch.shape
    total_rows = local_rows * lax.axis_size(("rows", "grp"))
    rows_place = lax.axis_index("rows")
    y = lax.axis_index("grp")
    core = lax.rem(rows_place, CORES)
    z = lax.rem(lax.div(rows_place, CORES), ZS)
    x = lax.div(rows_place, CORES * ZS)
    z_odd, z_pair = lax.rem(z, 2), lax.div(z, 2)
    place = jnp.stack([core, y, x]).astype(jnp.int32)
    tie = lax.optimization_barrier

    half = shard // CORES
    mine = cut(sketch, core, CORES, 0)
    arrived = [to_y(mine, step) for step in ORDER]
    passed = [to_core(value) for value in arrived]

    def part(start, value):
        strip = lax.dynamic_slice_in_dim(matrix, start, value.shape[0], axis=1)
        return jnp.dot(strip, value, preferred_element_type=jnp.float32)

    sketched = part(y * shard, sketch)
    for step, near, far in zip(ORDER, arrived, passed):
        source = (y ^ step) * shard
        sketched = sketched + part(source + core * half, near)
        sketched = sketched + part(source + (1 - core) * half, far)

    keep, send, stack = gram_pieces(place, sketched, (columns,))

    strips = []

    def strips_behind(count, *done):
        for _ in range(count):
            strips.append(product(place, stack, matrix, SEND[len(strips)]))
        tied, strips[-count:] = tie((done, strips[-count:]))
        return tied

    (other,) = strips_behind(2, to_core(send))
    summed = cut(keep, y, YS, 0) + cut(other, y, YS, 0)
    one, three, two = strips_behind(
        1,
        *[to_y(cut(keep, y ^ step, YS, 0) + cut(other, y ^ step, YS, 0), step) for step in ORDER],
    )
    summed = (summed + two) + (one + three)
    one, three, two = strips_behind(1, *[to_x(summed, step) for step in ORDER])
    summed = (summed + two) + (one + three)
    others = [to_core(sent) for _, sent in strips]
    summed = summed + to_z_pair(summed)
    summed, others = tie((summed, others))
    chunks_x, chunks_y = merge(place, [kept for kept, _ in strips], others)
    moved = [to_z(summed, step) for step in FAR_FIRST]
    (two, one, three), chunks_x, chunks_y = tie((moved, chunks_x, chunks_y))
    chunks_x = list(chunks_x)
    summed = (summed + two) + (one + three)
    pieces = [summed] + [to_y(summed, step) for step in ORDER]
    pieces = pieces + [to_core(value) for value in pieces]

    chunks_x[2:], chunks_y, pieces = tie((chunks_x[2:], chunks_y, pieces))
    moved_x = [to_x(chunk, step) for chunk, step in zip(chunks_x, ORDER)]
    moved_y = [to_y(chunk, step) for chunk, step in zip(chunks_y, ORDER)]
    root_rows = math.sqrt(total_rows)
    begun = factor_begin(place, pieces, columns, root_rows, 2)
    moved_y[:2], begun = tie((moved_y[:2], begun))
    triangle, inverse = factor_end(begun, moved_y[0], columns, root_rows, 2)
    moved_x, moved_y, _ = tie((moved_x, moved_y, inverse))
    over_x = chunks_x[3] + sum(moved_x)
    over_y = (chunks_y[3] + sum(moved_y)).reshape(XS, -1, columns // 2)
    over_x = scatter_sum(over_x, y, YS, to_y)
    over_y = over_y[3] + sum(to_x(over_y[at], step) for at, step in enumerate(ORDER))
    both = jnp.concatenate([over_x, over_y], axis=1)
    own = both.shape[0] // ZS
    both = both.reshape(ZS // 2, 2, own, columns)

    def parity(index):
        return lax.dynamic_index_in_dim(both, index, 1, keepdims=False)

    def through(value, precision):
        return lax.dot_general(
            value,
            inverse,
            (((1,), (1,)), ((), ())),
            precision=precision,
            preferred_element_type=jnp.float32,
        )

    basis_block = through(sketched, lax.Precision.HIGH).astype(jnp.bfloat16)
    other, basis_block = tie((to_z_pair(parity(1 - z_odd)), basis_block))
    both = parity(z_odd) + other
    strip = scatter_sum(both, z_pair, ZS // 2, to_z, order=FAR_FIRST).reshape(own, columns)
    projected = through(strip, lax.Precision.HIGH) * (math.sqrt(width) / total_rows)
    return (basis_block, triangle, projected)


def solution(mesh):
    return jax.shard_map(
        on_device,
        mesh=mesh,
        in_specs=(P(("rows", "grp"), None), P("grp", None)),
        out_specs=(P(("rows", "grp"), None), P(), P(("rows", "grp"), None)),
        check_vma=False,
    )
```
